32 devices in a mesh: ctx: 4 (over x, core), tsp: 4 (over z), dp: 2 (over y).
Axes of the slice: x: 2, y: 2, z: 4, core: 2. Of those that a mesh axis runs over, the one named last changes fastest.
Arguments:
- queries: bfloat16 [2, 2048, 2048], P('dp', 'ctx', 'tsp'), may hold values from -6 to 6
- keys: bfloat16 [2, 2048, 2048], P('dp', 'ctx', 'tsp'), may hold values from -6 to 6
- values: bfloat16 [2, 2048, 2048], P('dp', 'ctx', 'tsp'), may hold values from -6 to 6
- attn_out: bfloat16 [2, 2048, 2048], P('dp', 'ctx', 'tsp'), may hold values from -6 to 6
- out_grad: bfloat16 [2, 2048, 4096], P('dp', ('ctx', 'tsp')), may hold values from -3 to 3
- out_weight: bfloat16 [4096, 2048], P('ctx', 'tsp'), may hold values from -0.09375 to 0.09375
- block_mask: int32 [2, 4, 8, 8], P('dp', 'ctx'), may hold values 0 or 1
Outputs:
- query_grads: bfloat16 [2, 2048, 2048], P('dp', 'ctx', 'tsp')
- key_grads: bfloat16 [2, 2048, 2048], P('dp', 'ctx', 'tsp')
- value_grads: bfloat16 [2, 2048, 2048], P('dp', 'ctx', 'tsp')
- weight_grad: float32 [4096, 2048], P('ctx', 'tsp')
The draws below stay inside these ranges and needn't reach their ends.
Inputs may be any that keep to these rules, and one draw needn't show every extreme that they name: `block_mask`: 1 lets a key block feed a later query block of the same group.
All inputs are finite; a program needn't handle non-finite values.
Results may differ from the reference program's by a relative error of at most 0.0058.
Values may be sent and summed in bfloat16 or wider, within the bound.
No kernel may reach another device: no remote copies, remote signals or barrier semaphores. Data moves between devices by JAX's collectives and lax.ppermute only.
A program may use at most 128 MiB of HBM per device.

```python
import math
import jax
import jax.numpy as jnp
from jax import lax

D = 4096
HEADS = 16
HEAD = 128
BLK = 64
GROUP = 512
NB = 8
GROUPS = 4
SEQ = 2048
BATCH = 2
HD = 2048


def with_ends(values, rng, smallest, high):
    place = [jax.random.randint(jax.random.fold_in(rng, axis), (), 0, length) for axis, length in enumerate(values.shape)]
    longest = values.shape.index(max(values.shape))
    neighbour = place[:longest] + [(place[longest] + 1) % values.shape[longest]] + place[longest + 1:]
    return values.at[tuple(place)].set(smallest).at[tuple(neighbour)].set(high)


def strengthened(values, rng, source, target, parts, factor):
    def block_of(position):
        return (jnp.arange(values.shape[position]) // (values.shape[position] // parts)).reshape((-1,) + (1,) * (values.ndim - 1 - position))

    near = jax.random.permutation(rng, parts)[block_of(target)]
    other_side = (block_of(target) + parts // 2) % parts
    return jnp.where((block_of(source) == near) | (block_of(source) == other_side), factor * values, values)


def level_of(own_key, dims, split, least, largest):
    level = 1.0
    for axis_at, blocks in split:
        steps = jax.random.uniform(jax.random.fold_in(jax.random.fold_in(own_key, 6), axis_at), (blocks,), jnp.float32, least / len(split), largest / len(split))
        level = level * jnp.repeat(jnp.exp(steps), dims[axis_at] // blocks).reshape((-1,) + (1,) * (len(dims) - 1 - axis_at))
    return level


def gaussian(rng, extent, scale, bound, split=(), held_as=jnp.bfloat16):
    result = scale * jax.random.normal(rng, extent, jnp.float32)
    if split:
        result = result * level_of(rng, extent, split, -0.22, 0.18)
    return jnp.clip(result, -bound, bound).astype(held_as)


def noise_with(rng, shape, scale, reach, pieces, heavy, kind=jnp.bfloat16):
    entries = scale * jax.random.normal(rng, shape, jnp.float32)
    if pieces:
        entries = entries * level_of(rng, shape, pieces, -0.22, 0.18)
    return jnp.clip(strengthened(entries, jax.random.fold_in(rng, 3), *heavy), -reach, reach).astype(kind)


def setup_inputs(seed: int = 0) -> dict:
    key_list = jax.random.split(jax.random.key(seed), 8)
    return {
        "queries": gaussian(key_list[0], (BATCH, SEQ, HD), 1.0, 6.0, ((0, 2), (1, 4), (2, 4))),
        "keys": gaussian(key_list[1], (BATCH, SEQ, HD), 1.0, 6.0, ((0, 2), (1, 4), (2, 4))),
        "values": gaussian(key_list[2], (BATCH, SEQ, HD), 1.0, 6.0, ((0, 2), (1, 4), (2, 4))),
        "attn_out": gaussian(key_list[3], (BATCH, SEQ, HD), 1.0, 6.0, ((0, 2), (1, 4), (2, 4))),
        "out_grad": noise_with(key_list[4], (BATCH, SEQ, D), 0.5, 3.0, ((0, 2), (1, 16)), (1, 2, 16, 2.0)),
        "out_weight": gaussian(key_list[5], (D, HD), D ** -0.5, 0.09375, ((0, 4), (1, 4))),
        "block_mask": with_ends((jax.random.randint(key_list[6], (BATCH, GROUPS, NB, NB), 0, 2) < 1).astype(jnp.int32), jax.random.fold_in(key_list[6], 1), 0, 1),
    }


def allowed_pairs(block_table):
    blocks = block_table.shape[0]
    length = blocks * BLK
    wide_table = jnp.broadcast_to(block_table[:, None, :, None], (blocks, BLK, blocks, BLK)).reshape(length, length)
    row_pos = jnp.arange(length)[:, None]
    col_pos = jnp.arange(length)[None, :]
    row_blk = row_pos // BLK
    col_blk = col_pos // BLK
    return (row_blk > col_blk) & (wide_table == 1) | (row_blk == col_blk) & (row_pos >= col_pos)

def reference(queries, keys, values, attn_out, out_grad, out_weight, block_mask):
    f32 = jnp.float32
    score_scale = 1.0 / math.sqrt(HEAD * SEQ)
    flat_grad = out_grad.reshape(BATCH * SEQ, D)
    out_grads = jnp.dot(flat_grad, out_weight, preferred_element_type=f32).astype(jnp.bfloat16)
    weight_grad = jnp.dot(flat_grad.T, attn_out.reshape(BATCH * SEQ, HEADS * HEAD), preferred_element_type=f32) / math.sqrt(BATCH * SEQ)
    shape_five = (BATCH, GROUPS, GROUP, HEADS, HEAD)
    query_five = queries.reshape(shape_five)
    key_five = keys.reshape(shape_five)
    value_five = values.reshape(shape_five)
    grad_five = out_grads.reshape(shape_five)
    key_value = jnp.einsum('bcthd,bcthe->bchde', key_five.astype(f32), value_five.astype(f32))
    query_grad = jnp.einsum('bcthd,bcthe->bchde', query_five.astype(f32), grad_five.astype(f32))
    earlier_sum = jnp.cumsum(key_value, axis=1) - key_value
    later_sum = jnp.flip(jnp.cumsum(jnp.flip(query_grad, 1), axis=1), 1) - query_grad
    prev_state = (earlier_sum * score_scale).astype(jnp.bfloat16)
    later_state = (later_sum * score_scale).astype(jnp.bfloat16)
    items = BATCH * GROUPS
    shape_four = (items, GROUP, HEADS, HEAD)
    state_shape = (items, HEADS, HEAD, HEAD)
    stacked = (query_five.reshape(shape_four), key_five.reshape(shape_four), value_five.reshape(shape_four), grad_five.reshape(shape_four), prev_state.reshape(state_shape), later_state.reshape(state_shape), block_mask.reshape(items, NB, NB))

    def one_group(item):
        query_here, key_here, value_here, grad_here, prev_here, later_here, table_here = item
        allowed = allowed_pairs(table_here)
        query_f = query_here.astype(f32)
        key_f = key_here.astype(f32)
        value_f = value_here.astype(f32)
        grad_f = grad_here.astype(f32)
        scores = jnp.einsum('thd,shd->hts', query_f, key_f) * score_scale
        score_weights = jnp.where(allowed[None], scores, 0.0).astype(jnp.bfloat16).astype(f32)
        mixing = jnp.einsum('the,she->hts', grad_f, value_f) * score_scale
        grad_weights = jnp.where(allowed[None], mixing, 0.0).astype(jnp.bfloat16).astype(f32)
        prev_f = prev_here.astype(f32)
        later_f = later_here.astype(f32)
        query_out = jnp.einsum('hts,shd->thd', grad_weights, key_f) + jnp.einsum('the,hde->thd', grad_f, prev_f)
        key_out = jnp.einsum('hts,thd->shd', grad_weights, query_f) + jnp.einsum('she,hde->shd', value_f, later_f)
        value_out = jnp.einsum('hts,the->she', score_weights, grad_f) + jnp.einsum('shd,hde->she', key_f, later_f)
        return (query_out.astype(jnp.bfloat16), key_out.astype(jnp.bfloat16), value_out.astype(jnp.bfloat16))
    query_grads, key_grads, value_grads = lax.map(one_group, stacked)
    out_shape = (BATCH, SEQ, HEADS * HEAD)
    return (query_grads.reshape(out_shape), key_grads.reshape(out_shape), value_grads.reshape(out_shape), weight_grad)
```

```python
import functools
import math

import jax
import jax.numpy as jnp
from jax import lax
from jax.experimental import pallas as pl
from jax.experimental.pallas import tpu as pltpu
from jax.sharding import PartitionSpec as P

HEAD = 128
BLK = 64
CHUNKS = 4
F32 = jnp.float32
BF16 = jnp.bfloat16
NT = (((1,), (1,)), ((), ()))
NN = (((1,), (0,)), ((), ()))
TN = (((0,), (0,)), ((), ()))
VMEM_LIMIT = 48 * 1024 * 1024


def mm(a, b, dims):
    return lax.dot_general(a, b, dims, preferred_element_type=F32)


def params():
    return pltpu.CompilerParams(vmem_limit_bytes=VMEM_LIMIT)


def allowed_pairs(block_table):
    blocks = block_table.shape[0]
    length = blocks * BLK
    wide_table = jnp.broadcast_to(
        block_table[:, None, :, None], (blocks, BLK, blocks, BLK)
    ).reshape(length, length)
    row_pos = jnp.arange(length)[:, None]
    col_pos = jnp.arange(length)[None, :]
    row_blk = row_pos // BLK
    col_blk = col_pos // BLK
    return (row_blk > col_blk) & (wide_table == 1) | (row_blk == col_blk) & (row_pos >= col_pos)


def bits_of(count):
    return [1 << b for b in range(count.bit_length() - 1)]


def reversed_order(count):
    order = [0]
    for bit in reversed(bits_of(count)):
        order = order + [j | bit for j in order]
    width = count.bit_length() - 1
    return [int(format(p, "b").zfill(width)[::-1], 2) if width else 0 for p in range(count)]


def swap(array, axis, bit):
    count = lax.axis_size(axis)
    return lax.ppermute(array, axis, [(i, i ^ bit) for i in range(count)])


def scan_states(state, axis, later, sent):
    here = lax.axis_index(axis)
    outside, total = jnp.zeros_like(state), state
    bits = bits_of(lax.axis_size(axis))
    for bit in bits:
        coming = swap(total.astype(sent), axis, bit).astype(F32)
        high = (here & bit) != 0
        outside = outside + jnp.where(high != later, coming, 0.0)
        if bit != bits[-1]:
            total = total + coming
    return outside


def early_kernel(q_ref, k_ref, v_ref, maskt_ref, st_ref, kv_ref):
    k = k_ref[...]
    st_ref[0] = (mm(k, q_ref[...], NT) * maskt_ref[...]).astype(BF16)
    kv_ref[0] = mm(k, v_ref[...], TN)


def early(q, k, v, maskt):
    length, width = q.shape
    heads = width // HEAD
    one = pl.BlockSpec((length, HEAD), lambda h: (0, h))
    return pl.pallas_call(
        early_kernel,
        grid=(heads,),
        in_specs=[one, one, one, pl.BlockSpec((length, length), lambda h: (0, 0))],
        out_specs=[
            pl.BlockSpec((1, length, length), lambda h: (h, 0, 0)),
            pl.BlockSpec((1, HEAD, HEAD), lambda h: (h, 0, 0)),
        ],
        out_shape=[
            jax.ShapeDtypeStruct((heads, length, length), BF16),
            jax.ShapeDtypeStruct((heads, HEAD, HEAD), F32),
        ],
        compiler_params=params(),
        name="early",
    )(q, k, v, maskt)


def late_kernel(q_ref, k_ref, v_ref, g_ref, st_ref, prev_ref, mask_ref, maskt_ref, dq_ref, dk_ref, dv_ref):
    q, k, v, g = q_ref[...], k_ref[...], v_ref[...], g_ref[...]
    m = (mm(g, v, NT) * mask_ref[...]).astype(BF16)
    dq_ref[...] = (mm(m, k, NN) + mm(g, prev_ref[0], NT)).astype(BF16)
    mt = (mm(v, g, NT) * maskt_ref[...]).astype(BF16)
    dk_ref[...] = mm(mt, q, NN)
    dv_ref[...] = mm(st_ref[0], g, NN)


def late(q, k, v, g, st, prev, mask, maskt):
    length, width = q.shape
    heads = width // HEAD
    one = pl.BlockSpec((length, HEAD), lambda h: (0, h))
    full = pl.BlockSpec((length, length), lambda h: (0, 0))
    return pl.pallas_call(
        late_kernel,
        grid=(heads,),
        in_specs=[
            one, one, one, one,
            pl.BlockSpec((1, length, length), lambda h: (h, 0, 0)),
            pl.BlockSpec((1, HEAD, HEAD), lambda h: (h, 0, 0)),
            full, full,
        ],
        out_specs=[one, one, one],
        out_shape=[
            jax.ShapeDtypeStruct((length, width), BF16),
            jax.ShapeDtypeStruct((length, width), F32),
            jax.ShapeDtypeStruct((length, width), F32),
        ],
        compiler_params=params(),
        name="late",
    )(q, k, v, g, st, prev, mask, maskt)


def final_kernel(k_ref, v_ref, later_ref, dkp_ref, dvp_ref, dk_ref, dv_ref):
    s = later_ref[0]
    dk_ref[...] = (dkp_ref[...] + mm(v_ref[...], s, NT)).astype(BF16)
    dv_ref[...] = (dvp_ref[...] + mm(k_ref[...], s, NN)).astype(BF16)


def final(k, v, later, dkp, dvp):
    length, width = k.shape
    heads = width // HEAD
    one = pl.BlockSpec((length, HEAD), lambda h: (0, h))
    return pl.pallas_call(
        final_kernel,
        grid=(heads,),
        in_specs=[one, one, pl.BlockSpec((1, HEAD, HEAD), lambda h: (h, 0, 0)), one, one],
        out_specs=[one, one],
        out_shape=[jax.ShapeDtypeStruct((length, width), BF16)] * 2,
        compiler_params=params(),
        name="final",
    )(k, v, later, dkp, dvp)


def fold_kernel(chunk, turns, parts, norm, first, last, *refs):
    refs = list(refs)
    z_ref, own_ref = refs.pop(0), refs.pop(0)
    right_refs = [refs.pop(0) for _ in range(turns - 1)]
    left_refs = [refs.pop(0) for _ in range(turns - 1)]
    w_refs = [refs.pop(0) for _ in range(parts)]
    opened_ref = refs.pop(0)
    acc_ref = None if first else refs.pop(0)
    q_ref = refs.pop(0) if last else None
    og_ref = refs.pop(0)
    qg_ref = refs.pop(0) if last else None
    keep_ref, send_ref, grad, weight, g_sem, w_sem = refs
    z = z_ref[0]
    rows = own_ref.shape[0]
    wide = own_ref.shape[1]
    part = wide // parts

    def place(ref, at):
        pltpu.make_async_copy(ref, grad.at[pl.ds(pl.multiple_of(at * rows, rows), rows)], g_sem).start()

    place(own_ref, z)
    for r in range(1, turns):
        pl.when(z >= r)(functools.partial(place, right_refs[r - 1], z - r))
        pl.when(z + r < turns)(functools.partial(place, left_refs[r - 1], z + r))
    for p in range(parts):
        pltpu.make_async_copy(
            w_refs[p].at[pl.ds(chunk * part, part)], weight.at[pl.ds(p * part, part)], w_sem
        ).start()
    pltpu.make_async_copy(grad, grad, g_sem).wait()
    half = wide // 2
    step = 256
    opened = opened_ref[...]
    for f in range(0, wide, step):
        piece = mm(grad[:, f:f + step], opened, TN) * norm
        if f < half:
            keep_ref[f:f + step, :] = piece
        else:
            send_ref[f - half:f - half + step, :] = piece.astype(BF16)
    pltpu.make_async_copy(weight, weight, w_sem).wait()
    total = mm(grad[...], weight[...], NN)
    if not first:
        total = total + acc_ref[...]
    if last:
        total = total.astype(BF16)
        og_ref[...] = total
        for h in range(total.shape[1] // HEAD):
            at = slice(h * HEAD, (h + 1) * HEAD)
            qg_ref[h] = mm(q_ref[:, at], total[:, at], TN)
    else:
        og_ref[...] = total


def fold(chunk, z, own, rights, lefts, ws, opened, acc, q, norm):
    rows, wide = own.shape
    turns = len(rights) + 1
    length, width = opened.shape
    first, last = acc is None, q is not None
    anyspec = pl.BlockSpec(memory_space=pl.ANY)
    vmem = pl.BlockSpec(memory_space=pltpu.VMEM)
    args = [z, own, *rights, *lefts, *ws, opened]
    specs = [pl.BlockSpec(memory_space=pltpu.SMEM)] + [anyspec] * (len(args) - 2) + [vmem]
    if not first:
        args.append(acc)
        specs.append(vmem)
    if last:
        args.append(q)
        specs.append(vmem)
    outs = [jax.ShapeDtypeStruct((length, width), BF16 if last else F32)]
    if last:
        outs.append(jax.ShapeDtypeStruct((width // HEAD, HEAD, HEAD), F32))
    outs += [
        jax.ShapeDtypeStruct((wide // 2, width), F32),
        jax.ShapeDtypeStruct((wide // 2, width), BF16),
    ]
    return pl.pallas_call(
        functools.partial(fold_kernel, chunk, turns, len(ws), norm, first, last),
        in_specs=specs,
        out_specs=[vmem] * len(outs),
        out_shape=outs,
        scratch_shapes=[
            pltpu.VMEM((length, wide), BF16),
            pltpu.VMEM((wide, width), BF16),
            pltpu.SemaphoreType.DMA,
            pltpu.SemaphoreType.DMA,
        ],
        compiler_params=params(),
        name="fold",
    )(*args)


def shards(queries, keys, values, attn_out, out_grad, out_weight, block_mask):
    ctx, tsp = lax.axis_size("ctx"), lax.axis_size("tsp")
    _, group_len, width = queries.shape
    heads = width // HEAD
    seq_len = group_len * ctx
    sc = 1.0 / math.sqrt(HEAD * seq_len)
    norm = 1.0 / math.sqrt(seq_len * lax.axis_size("dp"))
    me, z = lax.axis_index("ctx"), lax.axis_index("tsp")
    q, k, v, opened = queries[0], keys[0], values[0], attn_out[0]
    grad = out_grad[0]
    rows, model = grad.shape
    order = reversed_order(ctx)
    block = model // ctx
    piece = block // CHUNKS

    own = []
    for c in range(CHUNKS):
        own.append(jnp.concatenate(
            [lax.dynamic_slice(grad, (0, (me ^ j) * block + c * piece), (rows, piece)) for j in order], axis=1))

    held = {0: out_weight}
    for bit in reversed(bits_of(ctx)):
        for j in list(held):
            held[j | bit] = swap(held[j], "ctx", bit)
    ws = [held[j] for j in order]

    merged = tsp >= 4

    def hop(array, r, right):
        if right:
            pairs = [(i, i + 1) for i in range(r - 1, tsp - 1)]
        else:
            pairs = [(i, i - 1) for i in range(1, tsp - r + 1)]
        return lax.ppermute(array, "tsp", pairs)

    rights = [[] for _ in range(CHUNKS)]
    lefts = [[] for _ in range(CHUNKS)]
    for wave in range(CHUNKS + tsp - 2):
        for r in range(1, tsp):
            c = wave - (r - 1)
            if not 0 <= c < CHUNKS:
                continue
            if merged and r == tsp - 1:
                both = jnp.where(z == tsp - 2, rights[c][-1], lefts[c][-1])
                got = lax.ppermute(both, "tsp", [(tsp - 2, tsp - 1), (1, 0)])
                rights[c].append(got)
                lefts[c].append(got)
            else:
                rights[c].append(hop(rights[c][-1] if r > 1 else own[c], r, True))
                lefts[c].append(hop(lefts[c][-1] if r > 1 else own[c], r, False))

    allowed = allowed_pairs(block_mask[0, 0])
    mask = jnp.where(allowed, sc, 0.0).astype(F32)
    maskt = mask.T
    st, kv = early(q, k, v, maskt)
    prev = (scan_states(kv, "ctx", False, F32) * sc).astype(BF16)

    acc = None
    zs = jnp.reshape(z, (1,)).astype(jnp.int32)
    done = []
    for c in range(CHUNKS):
        last = c == CHUNKS - 1
        got = fold(c, zs, own[c], rights[c], lefts[c], ws, opened, acc, q if last else None, norm)
        if last:
            acc, qg, keep, send = got
        else:
            acc, keep, send = got
        for bit in bits_of(ctx):
            coming = swap(send, "ctx", bit).astype(F32)
            total = keep + coming
            if total.shape[0] > piece:
                keep, send = total[: total.shape[0] // 2], total[total.shape[0] // 2:].astype(BF16)
        mine = total.astype(BF16)
        done.append((mine, lax.ppermute(mine, "dp", [(0, 1), (1, 0)])))
    og = acc
    later_sum = scan_states(qg, "ctx", True, BF16)
    dq, dkp, dvp = late(q, k, v, og, st, prev, mask, maskt)
    later = (later_sum * sc).astype(BF16)
    dk, dv = final(k, v, later, dkp, dvp)
    weight_grad = jnp.concatenate([a.astype(F32) + b.astype(F32) for a, b in done], axis=0)
    return dq[None], dk[None], dv[None], weight_grad


def solution(mesh):
    placed = (
        P("dp", "ctx", "tsp"),
        P("dp", "ctx", "tsp"),
        P("dp", "ctx", "tsp"),
        P("dp", "ctx", "tsp"),
        P("dp", ("ctx", "tsp"), None),
        P("ctx", "tsp"),
        P("dp", "ctx", None, None),
    )
    return jax.shard_map(
        shards,
        mesh=mesh,
        in_specs=placed,
        out_specs=(
            P("dp", "ctx", "tsp"),
            P("dp", "ctx", "tsp"),
            P("dp", "ctx", "tsp"),
            P("ctx", "tsp"),
        ),
        check_vma=False,
    )
```

```python
import functools
import math

import jax
import jax.numpy as jnp
from jax import lax
from jax.experimental import pallas as pl
from jax.experimental.pallas import tpu as pltpu
from jax.sharding import PartitionSpec as P

HEAD = 128
BLK = 64
EIGHTHS = (3, 2, 2, 1)
CORE_SENDS = (4, 4, 8, 1)
F32 = jnp.float32
BF16 = jnp.bfloat16
NT = (((1,), (1,)), ((), ()))
NN = (((1,), (0,)), ((), ()))
TN = (((0,), (0,)), ((), ()))
ANY = pl.BlockSpec(memory_space=pl.ANY)
SMEM = pl.BlockSpec(memory_space=pltpu.SMEM)
VMEM = pl.BlockSpec(memory_space=pltpu.VMEM)
HBM = pl.BlockSpec(memory_space=pltpu.HBM)


def mm(a, b, dims):
    return lax.dot_general(a, b, dims, preferred_element_type=F32)


def params(mebibytes=16):
    return pltpu.CompilerParams(vmem_limit_bytes=mebibytes * 1024 * 1024)


def bits_of(count):
    return [1 << b for b in range(count.bit_length() - 1)]


def reversed_order(count):
    width = count.bit_length() - 1
    return [int(format(p, "b").zfill(width)[::-1], 2) if width else 0 for p in range(count)]


def swap(array, axis, bit):
    count = lax.axis_size(axis)
    return lax.ppermute(array, axis, [(i, i ^ bit) for i in range(count)])


def in_hbm(*arrays):
    return [pltpu.with_memory_space_constraint(x, pltpu.HBM) for x in arrays]


def in_vmem(*arrays):
    return [pltpu.with_memory_space_constraint(x, pltpu.VMEM) for x in arrays]


def tie(array, *after):
    def kernel(*refs):
        pass

    return pl.pallas_call(
        kernel,
        in_specs=[ANY] * (1 + len(after)),
        out_specs=ANY,
        out_shape=jax.ShapeDtypeStruct(array.shape, array.dtype),
        input_output_aliases={0: 0},
        compiler_params=params(1),
        name="tie",
    )(array, *after)


def on_vmem(body, outs, arrays, after=(), name="on_vmem"):
    def kernel(*refs):
        body(*refs[:len(arrays)], *refs[len(arrays) + len(after):])

    return pl.pallas_call(
        kernel,
        in_specs=[VMEM] * len(arrays) + [ANY] * len(after),
        out_specs=[VMEM] * len(outs),
        out_shape=[pltpu.VMEM(shape, kind) for shape, kind in outs],
        compiler_params=params(),
        name=name,
    )(*in_vmem(*arrays), *after)


def load(pieces):
    count = len(pieces)

    def kernel(*refs):
        sources, targets, sems = refs[:count], refs[count:-1], refs[-1]
        copies = [
            pltpu.make_async_copy(source.at[pl.ds(first, rows)], target, sems.at[i])
            for i, (source, target, (_, first, rows)) in enumerate(zip(sources, targets, pieces))
        ]
        for copy in copies:
            copy.start()
        for copy in copies:
            copy.wait()

    return pl.pallas_call(
        kernel,
        in_specs=[HBM] * count,
        out_specs=[VMEM] * count,
        out_shape=[pltpu.VMEM((rows, x.shape[1]), x.dtype) for x, _, rows in pieces],
        scratch_shapes=[pltpu.SemaphoreType.DMA((count,))],
        compiler_params=params(1),
        name="load",
    )(*in_hbm(*[x for x, _, _ in pieces]))


def in_rows(array, count):
    rows = array.shape[0] // count

    def body(*refs):
        for i in range(count):
            refs[1 + i][...] = refs[0][i * rows:(i + 1) * rows, :]

    return on_vmem(body, [((rows, array.shape[1]), array.dtype)] * count, [array], name="in_rows")


def rows_of(refs, start, size):
    found, at = [], 0
    for ref in refs:
        low, high = max(start, at), min(start + size, at + ref.shape[0])
        if low < high:
            found.append(ref[low - at:high - at, :])
        at += ref.shape[0]
    return found[0] if len(found) == 1 else jnp.concatenate(found, axis=0)


def cut(whole, order, offsets, pieces):
    rows, model = whole.shape
    block = model // len(order)
    if pieces[-1] % 128:
        here = lax.axis_index("ctx")
        return [
            jnp.concatenate([lax.dynamic_slice(whole, (0, (here ^ j) * block + o), (rows, p)) for j in order], axis=1)
            for o, p in zip(offsets, pieces)
        ]

    def kernel(source, *refs):
        targets, sems = refs[:-1], refs[-1]
        here = lax.axis_index("ctx")
        for i, (offset, piece) in enumerate(zip(offsets, pieces)):
            for p, j in enumerate(order):
                at = pl.multiple_of((here ^ j) * block + offset, 128)
                pltpu.make_async_copy(
                    source.at[:, pl.ds(at, piece)], targets[i].at[:, pl.ds(p * piece, piece)], sems.at[i]
                ).start()
        for i, target in enumerate(targets):
            pltpu.make_async_copy(target, target, sems.at[i]).wait()

    return list(pl.pallas_call(
        kernel,
        in_specs=[HBM],
        out_specs=[VMEM] * len(pieces),
        out_shape=[pltpu.VMEM((rows, piece * len(order)), whole.dtype) for piece in pieces],
        scratch_shapes=[pltpu.SemaphoreType.DMA((len(pieces),))],
        compiler_params=params(1),
        name="cut",
    )(*in_hbm(whole)))


def scan_states(state, sc, later):
    shape = state.shape
    bits = bits_of(lax.axis_size("ctx"))
    total, came = state, []
    for bit in bits:
        if bit != bits[0]:
            total, = on_vmem(add_kernel, [(shape, total.dtype)], [total, came[-1]], name="add")
        came.append(swap(total, "ctx", bit))

    def body(*refs):
        here = lax.axis_index("ctx")
        sums = jnp.zeros(shape, F32)
        for bit, ref in zip(bits, refs):
            high = ((here & bit) != 0).astype(F32)
            sums = sums + ref[...].astype(F32) * ((1.0 - high) if later else high)
        refs[-1][...] = (sums * sc).astype(BF16)

    return on_vmem(body, [(shape, BF16)], came, name="states")[0], total


def add_kernel(a_ref, b_ref, out_ref):
    out_ref[...] = (a_ref[...].astype(F32) + b_ref[...].astype(F32)).astype(out_ref.dtype)


def spread(table, length):
    blocks = table.shape[0]
    row = lax.broadcasted_iota(jnp.int32, (length, blocks), 0) // BLK
    pick = (row == lax.broadcasted_iota(jnp.int32, (length, blocks), 1)).astype(BF16)
    chosen = mm(pick, (table == 1).astype(BF16), NN).astype(BF16)
    return mm(chosen, pick, NT)


def heads_of(ref):
    return [slice(h * HEAD, (h + 1) * HEAD) for h in range(ref.shape[1] // HEAD)]


def early(q, k, v, table, sc):
    length, width = q.shape
    heads = width // HEAD

    def body(table_ref, q_ref, k_ref, v_ref, mask_ref, s_ref, kv_ref):
        wide = spread(table_ref[...], length)
        row = lax.broadcasted_iota(jnp.int32, (length, length), 0)
        col = lax.broadcasted_iota(jnp.int32, (length, length), 1)
        inside = (row // BLK == col // BLK) & (row >= col)
        before = (row // BLK > col // BLK) & (wide > 0.5)
        mask_ref[...] = jnp.where(inside | before, sc, 0.0)
        for h, at in enumerate(heads_of(q_ref)):
            k_here = k_ref[:, at]
            s_ref[h] = (mm(q_ref[:, at], k_here, NT) * mask_ref[...]).astype(BF16)
            kv_ref[h] = mm(k_here, v_ref[:, at], TN)

    return on_vmem(
        body,
        [((length, length), F32), ((heads, length, length), BF16), ((heads, HEAD, HEAD), F32)],
        [table, q, k, v],
        name="early",
    )


def late_kernel(q_ref, k_ref, v_ref, g_ref, s_ref, prev_ref, mask_ref, *refs):
    dq_ref, dkp_ref, dvp_ref, dq, sem = refs[-5:]
    half = q_ref.shape[0] // 2
    lo, hi = slice(0, half), slice(half, 2 * half)
    for h, at in enumerate(heads_of(q_ref)):
        q, k, v, g = q_ref[:, at], k_ref[:, at], v_ref[:, at], g_ref[:, at]

        def weights(rows, cols):
            return (mm(g[rows], v[cols], NT) * mask_ref[rows, cols]).astype(BF16)

        m00, m10, m11 = weights(lo, lo), weights(hi, lo), weights(hi, hi)
        from_state = mm(g, prev_ref[h], NT)
        dq[lo, at] = (mm(m00, k[lo], NN) + from_state[lo]).astype(BF16)
        dq[hi, at] = (mm(m10, k[lo], NN) + mm(m11, k[hi], NN) + from_state[hi]).astype(BF16)
        dkp_ref[lo, at] = mm(m00, q[lo], TN) + mm(m10, q[hi], TN)
        dkp_ref[hi, at] = mm(m11, q[hi], TN)
        dvp_ref[lo, at] = mm(s_ref[h, :, lo], g, TN)
        dvp_ref[hi, at] = mm(s_ref[h, hi, hi], g[hi], TN)
    copy = pltpu.make_async_copy(dq, dq_ref, sem)
    copy.start()
    copy.wait()


def late(q, k, v, g, s, prev, mask, after):
    shape = q.shape
    return pl.pallas_call(
        late_kernel,
        in_specs=[VMEM] * 7 + [ANY] * len(after),
        out_specs=[HBM, VMEM, VMEM],
        out_shape=[pltpu.HBM(shape, BF16), pltpu.VMEM(shape, F32), pltpu.VMEM(shape, F32)],
        scratch_shapes=[pltpu.VMEM(shape, BF16), pltpu.SemaphoreType.DMA],
        compiler_params=params(),
        name="late",
    )(*in_vmem(q, k, v, g, s, prev, mask), *after)


def final_kernel(k_ref, v_ref, later_ref, dkp_ref, dvp_ref, *refs):
    dk_ref, dv_ref, dk, dv, sems = refs[-5:]
    for h, at in enumerate(heads_of(k_ref)):
        dk[:, at] = (dkp_ref[:, at] + mm(v_ref[:, at], later_ref[h], NT)).astype(BF16)
    copy_k = pltpu.make_async_copy(dk, dk_ref, sems.at[0])
    copy_k.start()
    for h, at in enumerate(heads_of(k_ref)):
        dv[:, at] = (dvp_ref[:, at] + mm(k_ref[:, at], later_ref[h], NN)).astype(BF16)
    copy_v = pltpu.make_async_copy(dv, dv_ref, sems.at[1])
    copy_v.start()
    copy_k.wait()
    copy_v.wait()


def final(k, v, later, dkp, dvp, after):
    shape = k.shape
    return pl.pallas_call(
        final_kernel,
        in_specs=[VMEM] * 5 + [ANY] * len(after),
        out_specs=[HBM, HBM],
        out_shape=[pltpu.HBM(shape, BF16)] * 2,
        scratch_shapes=[pltpu.VMEM(shape, BF16)] * 2 + [pltpu.SemaphoreType.DMA((2,))],
        compiler_params=params(),
        name="final",
    )(*in_vmem(k, v, later, dkp, dvp), *after)


def fold(blocks, opened, norm, ws, products, acc, q, sends, after=()):
    own, a, b1, c1, b2, c2 = blocks
    rows, wide = own.shape
    length, width = opened.shape
    half = wide // 2
    last, whole = q is not None, not products
    kept = [g for g, _ in products if g is not None]
    flat_ws = [x for w in ws for x in w] if products else []
    arrays = [own, a, b1, c1, b2, *c2, opened, *kept, *flat_ws]
    arrays += ([] if acc is None else [acc]) + ([q] if last else [])
    outs = [((half, width), F32)] + [((half // sends, width), BF16)] * sends
    if whole:
        outs.append(((length, wide), BF16))
    else:
        outs.append(((length, width), BF16 if last else F32))
    if last:
        outs.append(((width // HEAD, HEAD, HEAD), BF16))

    def kernel(*refs):
        refs = list(refs)
        own_ref, a_ref, b1_ref, c1_ref, b2_ref = [refs.pop(0) for _ in range(5)]
        c2_refs = [refs.pop(0) for _ in c2]
        opened_ref = refs.pop(0)
        kept_refs = [refs.pop(0) for _ in kept]
        w_refs = [[refs.pop(0) for _ in w] for w in ws] if products else []
        acc_ref = None if acc is None else refs.pop(0)
        q_ref = refs.pop(0) if last else None
        del refs[:len(after)]
        keep_ref = refs.pop(0)
        send_refs = [refs.pop(0) for _ in range(sends)]
        third_ref = refs.pop(0)
        qg_ref = refs.pop(0) if last else None
        grad = third_ref if whole else refs.pop(0)
        here = lax.axis_index("tsp")

        def place(ref, at, under=0):
            count = ref.shape[0]
            grad[pl.ds(pl.multiple_of(at * rows + under, count), count), :] = ref[...]

        at_end = (here == 0) | (here == 3)
        near, far = jnp.where(here < 2, 2, 1), jnp.where(here < 2, 3, 0)
        place(own_ref, here)
        place(a_ref, here ^ 1)

        @pl.when(at_end)
        def _():
            place(c1_ref, near)
            for i, ref in enumerate(c2_refs):
                place(ref, far, i * ref.shape[0])

        @pl.when(jnp.logical_not(at_end))
        def _():
            place(b1_ref, near)
            place(b2_ref, far)

        sent = (mm(grad[:, half:], opened_ref[...], TN) * norm).astype(BF16)
        for i, ref in enumerate(send_refs):
            ref[...] = sent[i * ref.shape[0]:(i + 1) * ref.shape[0], :]
        keep_ref[...] = mm(grad[:, :half], opened_ref[...], TN) * norm
        if whole:
            return
        total = None if acc is None else acc_ref[...]
        for g, start in products:
            source = grad if g is None else kept_refs.pop(0)
            piece = source.shape[1] // len(ws)
            rows_of_w = jnp.concatenate([rows_of(refs_here, start, piece) for refs_here in w_refs], axis=0)
            term = mm(source[...], rows_of_w, NN)
            total = term if total is None else total + term
        third_ref[...] = total.astype(third_ref.dtype)
        if last:
            for h, at in enumerate(heads_of(third_ref)):
                qg_ref[h] = mm(q_ref[:, at], third_ref[:, at], TN).astype(BF16)

    return pl.pallas_call(
        kernel,
        in_specs=[VMEM] * len(arrays) + [ANY] * len(after),
        out_specs=[VMEM] * len(outs),
        out_shape=[pltpu.VMEM(shape, kind) for shape, kind in outs],
        scratch_shapes=[] if whole else [pltpu.VMEM((length, wide), BF16)],
        compiler_params=params(),
        name="fold",
    )(*in_vmem(*arrays), *after)


def scatter_step(keep, sends, bit):
    came = [swap(x, "ctx", bit) for x in sends]
    half, width = keep.shape[0] // 2, keep.shape[1]

    def body(keep_ref, *refs):
        first_ref, second_ref = refs[-2:]
        came_refs = refs[:-2]
        first_ref[...] = keep_ref[:half, :] + rows_of(came_refs, 0, half).astype(F32)
        second_ref[...] = (keep_ref[half:, :] + rows_of(came_refs, half, half).astype(F32)).astype(BF16)

    return on_vmem(
        body, [((half, width), F32), ((half, width), BF16)], [keep, *came], name="split")


def finish(mine, came, offset, length, target):
    rows, width = mine.shape

    def kernel(*refs):
        mine_ref, came_ref = refs[:2]
        out_ref, total, sem = refs[-3:]
        total[...] = mine_ref[...].astype(F32) + came_ref[...].astype(F32)
        copy = pltpu.make_async_copy(total, out_ref.at[pl.ds(offset, rows)], sem)
        copy.start()
        copy.wait()

    extra = [] if target is None else [target]
    return pl.pallas_call(
        kernel,
        in_specs=[VMEM] * 2 + [HBM] * len(extra),
        out_specs=HBM,
        out_shape=pltpu.HBM((length, width), F32),
        input_output_aliases={} if target is None else {2: 0},
        scratch_shapes=[pltpu.VMEM((rows, width), F32), pltpu.SemaphoreType.DMA],
        compiler_params=params(),
        name="finish",
    )(*in_vmem(mine, came), *extra)


def shards(queries, keys, values, attn_out, out_grad, out_weight, block_mask):
    ctx = lax.axis_size("ctx")
    assert lax.axis_size("tsp") == 4 and lax.axis_size("dp") == 2
    _, group_len, width = queries.shape
    seq_len = group_len * ctx
    sc = 1.0 / math.sqrt(HEAD * seq_len)
    norm = 1.0 / math.sqrt(seq_len * lax.axis_size("dp"))
    grad = out_grad[0]
    order = reversed_order(ctx)
    block = grad.shape[1] // ctx
    count = len(EIGHTHS)
    pieces = [block * e // 8 for e in EIGHTHS]
    offsets = [sum(pieces[:i]) for i in range(count)]
    bits = bits_of(ctx)
    top = bits[-1]

    def outer(x):
        return lax.ppermute(x, "tsp", [(0, 1), (1, 0), (2, 3), (3, 2)])

    def inner(x):
        return lax.ppermute(x, "tsp", [(1, 2), (2, 1)])

    def to_ends(x):
        return lax.ppermute(x, "tsp", [(1, 0), (2, 3)])

    def other(x):
        return lax.ppermute(x, "dp", [(0, 1), (1, 0)])

    own = cut(grad, order, offsets, pieces)
    first = pieces[0]
    q, k, v, opened, w_here, w_low, w_high = load(
        [(x[0], 0, group_len) for x in (queries, keys, values, attn_out)]
        + [(out_weight, 0, block), (out_weight, 0, first), (out_weight, first, block - first)])
    a, b1, b2, c1, c2 = [[None] * count for _ in range(5)]

    def step_a(i, *after):
        if after:
            own[i] = tie(own[i], *after)
        a[i], b1[i] = outer(own[i]), inner(own[i])
        b2[i] = inner(a[i])

    def step_c1(i, *after):
        b1[i] = tie(b1[i], *after)
        c1[i] = to_ends(b1[i])

    def step_c2(i, *after, parts=1):
        b2[i] = tie(b2[i], *after)
        c2[i] = [to_ends(x) for x in (in_rows(b2[i], parts) if parts > 1 else [b2[i]])]

    step_a(0)
    step_a(1)

    held = {0: [w_here]}
    for bit in reversed(bits[1:]):
        for j in list(held):
            held[j | bit] = [swap(held[j][0], "ctx", bit)]
    for j in list(held):
        if j == 0:
            w_low = tie(w_low, a[1])
            held[j | bits[0]] = [swap(x, "ctx", bits[0]) for x in (w_low, w_high)]
        else:
            held[j | bits[0]] = [swap(x, "ctx", bits[0]) for x in in_rows(held[j][0], 4)]
    ws = [held[j] for j in order]

    mask, s, kv = early(q, k, v, block_mask[0, 0], sc)
    prev, _ = scan_states(kv, sc, False)

    step_c1(0, a[0])
    step_c2(0, a[1], held[bits[0]][0])
    step_a(2, c1[0])
    step_c1(1, *c2[0])
    step_c2(1, a[2], prev)
    step_a(3, c1[1])
    step_c1(2, *c2[1])
    step_c2(2, a[3])
    step_c1(3, c1[2])
    step_c2(3, *c2[2], parts=2)

    def add_top(keep, send, after=()):
        return on_vmem(
            add_kernel, [(keep.shape, BF16)], [keep, swap(send, "ctx", top)], after=after, name="mine")[0]

    keeps, sends, mine, theirs = [[None] * count for _ in range(4)]
    acc = kept = qg = None
    for i in range(count):
        last = i == count - 1
        products = [] if i == 0 else [(None, offsets[i])]
        if i == 1:
            products.insert(0, (kept, offsets[0]))
        keep, *rest = fold(
            (own[i], a[i], b1[i], c1[i], b2[i], c2[i]), opened, norm, ws, products, acc,
            q if last else None, CORE_SENDS[i])
        send, third, more = rest[:CORE_SENDS[i]], rest[CORE_SENDS[i]], rest[CORE_SENDS[i] + 1:]
        if i == 0:
            kept = third
        else:
            acc = third
        if last:
            qg = more[0]
        for bit in bits[:-1]:
            keep, send = scatter_step(keep, send, bit)
            send = [send]
        keeps[i], sends[i] = keep, send[0]
    og = acc
    for i in range(count - 2):
        mine[i] = add_top(keeps[i], sends[i])
        theirs[i] = other(mine[i])
    later, total_qg = scan_states(qg, sc, True)
    dq, dkp, dvp = late(q, k, v, og, s, prev, mask, (total_qg,))
    mine[-2] = add_top(keeps[-2], sends[-2], (dkp,))
    mine[-1] = add_top(keeps[-1], tie(sends[-1], *theirs[:-2]), (later,))
    theirs[-2], theirs[-1] = other(mine[-2]), other(mine[-1])
    dk, dv = final(k, v, later, dkp, dvp, ())
    grown = None
    for i in range(count):
        grown = finish(mine[i], theirs[i], offsets[i], block, grown)
    return dq[None], dk[None], dv[None], grown


def solution(mesh):
    placed = (
        P("dp", "ctx", "tsp"),
        P("dp", "ctx", "tsp"),
        P("dp", "ctx", "tsp"),
        P("dp", "ctx", "tsp"),
        P("dp", ("ctx", "tsp"), None),
        P("ctx", "tsp"),
        P("dp", "ctx", None, None),
    )
    return jax.shard_map(
        shards,
        mesh=mesh,
        in_specs=placed,
        out_specs=(
            P("dp", "ctx", "tsp"),
            P("dp", "ctx", "tsp"),
            P("dp", "ctx", "tsp"),
            P("ctx", "tsp"),
        ),
        check_vma=False,
    )
```

```python
import functools
import math

import jax
import jax.numpy as jnp
from jax import lax
from jax.experimental import pallas as pl
from jax.experimental.pallas import tpu as pltpu
from jax.sharding import PartitionSpec as P

HEAD = 128
BLK = 64
EIGHTHS = (3, 2, 2, 1)
GROUPS = ((0,), (1, 2, 3))
CORE_SENDS = (4, 4, 4, 2)
TOP_SENDS = (2, 1, 1, 1)
LAST_SENDS = (1, 1, 1, 1)
AFTER = {
    'cut': ('wcore',),
    'b2_1': ('c1_0',),
    'c1_1': ('b2_0',),
    'c2_2': ('prev',),
    'send_3': ('last_0', 'mine_1'),
    'late': ('qg',),
    'mine_3': ('later', 'late'),
    'fold_2': ('c2_3',),
    'fold_3': ('last_0',),
}
F32 = jnp.float32
BF16 = jnp.bfloat16
NT = (((1,), (1,)), ((), ()))
NN = (((1,), (0,)), ((), ()))
TN = (((0,), (0,)), ((), ()))
ANY = pl.BlockSpec(memory_space=pl.ANY)
SMEM = pl.BlockSpec(memory_space=pltpu.SMEM)
VMEM = pl.BlockSpec(memory_space=pltpu.VMEM)
HBM = pl.BlockSpec(memory_space=pltpu.HBM)


def mm(a, b, dims):
    return lax.dot_general(a, b, dims, preferred_element_type=F32)


def params(mebibytes=16):
    return pltpu.CompilerParams(vmem_limit_bytes=mebibytes * 1024 * 1024)


def bits_of(count):
    return [1 << b for b in range(count.bit_length() - 1)]


def reversed_order(count):
    width = count.bit_length() - 1
    return [int(format(p, "b").zfill(width)[::-1], 2) if width else 0 for p in range(count)]


def swap(array, axis, bit):
    count = lax.axis_size(axis)
    return lax.ppermute(array, axis, [(i, i ^ bit) for i in range(count)])


def in_hbm(*arrays):
    return [pltpu.with_memory_space_constraint(x, pltpu.HBM) for x in arrays]


def in_vmem(*arrays):
    return [pltpu.with_memory_space_constraint(x, pltpu.VMEM) for x in arrays]


def tie(array, *after):
    def kernel(*refs):
        pass

    return pl.pallas_call(
        kernel,
        in_specs=[ANY] * (1 + len(after)),
        out_specs=ANY,
        out_shape=jax.ShapeDtypeStruct(array.shape, array.dtype),
        input_output_aliases={0: 0},
        compiler_params=params(1),
        name="tie",
    )(array, *after)


def on_vmem(body, outs, arrays, after=(), name="on_vmem"):
    def kernel(*refs):
        body(*refs[:len(arrays)], *refs[len(arrays) + len(after):])

    return pl.pallas_call(
        kernel,
        in_specs=[VMEM] * len(arrays) + [ANY] * len(after),
        out_specs=[VMEM] * len(outs),
        out_shape=[pltpu.VMEM(shape, kind) for shape, kind in outs],
        compiler_params=params(),
        name=name,
    )(*in_vmem(*arrays), *after)


def load(pieces, cuts=()):
    sources = [x for x, _, _ in pieces] + [x for x, _ in cuts]
    shapes = [(rows, x.shape[1]) for x, _, rows in pieces]
    shapes += [(x.shape[0], sum(width for _, width in columns(0))) for x, columns in cuts]
    count = len(sources)

    def kernel(*refs):
        refs, targets, sems = refs[:count], refs[count:-1], refs[-1]
        for i, (_, first, rows) in enumerate(pieces):
            pltpu.make_async_copy(refs[i].at[pl.ds(first, rows)], targets[i], sems.at[i]).start()
        here = lax.axis_index("ctx")
        for i, (_, columns) in enumerate(cuts, len(pieces)):
            at = 0
            for start, width in columns(here):
                pltpu.make_async_copy(
                    refs[i].at[:, pl.ds(pl.multiple_of(start, 128), width)],
                    targets[i].at[:, pl.ds(at, width)], sems.at[i]
                ).start()
                at += width
        for i, target in enumerate(targets):
            pltpu.make_async_copy(target, target, sems.at[i]).wait()

    return pl.pallas_call(
        kernel,
        in_specs=[HBM] * count,
        out_specs=[VMEM] * count,
        out_shape=[pltpu.VMEM(shape, x.dtype) for shape, x in zip(shapes, sources)],
        scratch_shapes=[pltpu.SemaphoreType.DMA((count,))],
        compiler_params=params(1),
        name="load",
    )(*in_hbm(*sources))


def in_rows(array, count):
    rows = array.shape[0] // count

    def body(*refs):
        for i in range(count):
            refs[1 + i][...] = refs[0][i * rows:(i + 1) * rows, :]

    return on_vmem(body, [((rows, array.shape[1]), array.dtype)] * count, [array], name="in_rows")


def rows_of(refs, start, size):
    found, at = [], 0
    for ref in refs:
        low, high = max(start, at), min(start + size, at + ref.shape[0])
        if low < high:
            found.append(ref[low - at:high - at, :])
        at += ref.shape[0]
    return found[0] if len(found) == 1 else jnp.concatenate(found, axis=0)


def columns_of(group, order, block):
    return lambda here: [((here ^ j) * block + offset, piece) for offset, piece in group for j in order]


def cut(whole, order, groups, after=()):
    rows, model = whole.shape
    block = model // len(order)
    widths = [sum(piece for _, piece in group) * len(order) for group in groups]
    if any(piece % 128 for group in groups for _, piece in group):
        here = lax.axis_index("ctx")
        return [
            jnp.concatenate([
                lax.dynamic_slice(whole, (0, at), (rows, piece)) for at, piece in columns_of(group, order, block)(here)
            ], axis=1)
            for group in groups
        ]

    def body(source, *targets):
        here = lax.axis_index("ctx")
        for target, group in zip(targets, groups):
            column = 0
            for at, piece in columns_of(group, order, block)(here):
                target[:, column:column + piece] = source[:, pl.ds(pl.multiple_of(at, 128), piece)]
                column += piece

    return on_vmem(body, [((rows, width), whole.dtype) for width in widths], [whole], after=after, name="cut")


def scan_states(state, sc, later):
    shape = state.shape
    bits = bits_of(lax.axis_size("ctx"))
    total, came = state, []
    for bit in bits:
        if bit != bits[0]:
            total, = on_vmem(add_kernel, [(shape, total.dtype)], [total, came[-1]], name="add")
        came.append(swap(total, "ctx", bit))

    def body(*refs):
        here = lax.axis_index("ctx")
        sums = jnp.zeros(shape, F32)
        for bit, ref in zip(bits, refs):
            high = ((here & bit) != 0).astype(F32)
            sums = sums + ref[...].astype(F32) * ((1.0 - high) if later else high)
        refs[-1][...] = (sums * sc).astype(BF16)

    return on_vmem(body, [(shape, BF16)], came, name="states")[0], total


def add_kernel(a_ref, b_ref, out_ref):
    out_ref[...] = (a_ref[...].astype(F32) + b_ref[...].astype(F32)).astype(out_ref.dtype)


def spread(table, length):
    blocks = table.shape[0]
    row = lax.broadcasted_iota(jnp.int32, (length, blocks), 0) // BLK
    pick = (row == lax.broadcasted_iota(jnp.int32, (length, blocks), 1)).astype(BF16)
    chosen = mm(pick, (table == 1).astype(BF16), NN).astype(BF16)
    return mm(chosen, pick, NT)


def heads_of(ref):
    return [slice(h * HEAD, (h + 1) * HEAD) for h in range(ref.shape[1] // HEAD)]


def early(q, k, v, table, sc):
    length, width = q.shape
    heads = width // HEAD

    def body(table_ref, q_ref, k_ref, v_ref, mask_ref, s_ref, kv_ref):
        wide = spread(table_ref[...], length)
        row = lax.broadcasted_iota(jnp.int32, (length, length), 0)
        col = lax.broadcasted_iota(jnp.int32, (length, length), 1)
        inside = (row // BLK == col // BLK) & (row >= col)
        before = (row // BLK > col // BLK) & (wide > 0.5)
        mask_ref[...] = jnp.where(inside | before, sc, 0.0)
        for h, at in enumerate(heads_of(q_ref)):
            k_here = k_ref[:, at]
            s_ref[h] = (mm(q_ref[:, at], k_here, NT) * mask_ref[...]).astype(BF16)
            kv_ref[h] = mm(k_here, v_ref[:, at], TN).astype(BF16)

    return on_vmem(
        body,
        [((length, length), F32), ((heads, length, length), BF16), ((heads, HEAD, HEAD), BF16)],
        [table, q, k, v],
        name="early",
    )


def late_kernel(q_ref, k_ref, v_ref, g_ref, s_ref, prev_ref, mask_ref, *refs):
    dq_ref, dkp_ref, dvp_ref, dq, sem = refs[-5:]
    half = q_ref.shape[0] // 2
    lo, hi = slice(0, half), slice(half, 2 * half)
    for h, at in enumerate(heads_of(q_ref)):
        q, k, v, g = q_ref[:, at], k_ref[:, at], v_ref[:, at], g_ref[:, at]

        def weights(rows, cols):
            return (mm(g[rows], v[cols], NT) * mask_ref[rows, cols]).astype(BF16)

        m00, m10, m11 = weights(lo, lo), weights(hi, lo), weights(hi, hi)
        from_state = mm(g, prev_ref[h], NT)
        dq[lo, at] = (mm(m00, k[lo], NN) + from_state[lo]).astype(BF16)
        dq[hi, at] = (mm(m10, k[lo], NN) + mm(m11, k[hi], NN) + from_state[hi]).astype(BF16)
        dkp_ref[lo, at] = mm(m00, q[lo], TN) + mm(m10, q[hi], TN)
        dkp_ref[hi, at] = mm(m11, q[hi], TN)
        dvp_ref[lo, at] = mm(s_ref[h, :, lo], g, TN)
        dvp_ref[hi, at] = mm(s_ref[h, hi, hi], g[hi], TN)
    copy = pltpu.make_async_copy(dq, dq_ref, sem)
    copy.start()
    copy.wait()


def late(q, k, v, g, s, prev, mask, after):
    shape = q.shape
    return pl.pallas_call(
        late_kernel,
        in_specs=[VMEM] * 7 + [ANY] * len(after),
        out_specs=[HBM, VMEM, VMEM],
        out_shape=[pltpu.HBM(shape, BF16), pltpu.VMEM(shape, F32), pltpu.VMEM(shape, F32)],
        scratch_shapes=[pltpu.VMEM(shape, BF16), pltpu.SemaphoreType.DMA],
        compiler_params=params(),
        name="late",
    )(*in_vmem(q, k, v, g, s, prev, mask), *after)


def final_kernel(k_ref, v_ref, later_ref, dkp_ref, dvp_ref, *refs):
    dk_ref, dv_ref, dk, dv, sems = refs[-5:]
    for h, at in enumerate(heads_of(k_ref)):
        dk[:, at] = (dkp_ref[:, at] + mm(v_ref[:, at], later_ref[h], NT)).astype(BF16)
    copy_k = pltpu.make_async_copy(dk, dk_ref, sems.at[0])
    copy_k.start()
    for h, at in enumerate(heads_of(k_ref)):
        dv[:, at] = (dvp_ref[:, at] + mm(k_ref[:, at], later_ref[h], NN)).astype(BF16)
    copy_v = pltpu.make_async_copy(dv, dv_ref, sems.at[1])
    copy_v.start()
    copy_k.wait()
    copy_v.wait()


def final(k, v, later, dkp, dvp, after):
    shape = k.shape
    return pl.pallas_call(
        final_kernel,
        in_specs=[VMEM] * 5 + [ANY] * len(after),
        out_specs=[HBM, HBM],
        out_shape=[pltpu.HBM(shape, BF16)] * 2,
        scratch_shapes=[pltpu.VMEM(shape, BF16)] * 2 + [pltpu.SemaphoreType.DMA((2,))],
        compiler_params=params(),
        name="final",
    )(*in_vmem(k, v, later, dkp, dvp), *after)


def fold(blocks, opened, norm, ws, products, acc, q, sends, after=()):
    own, a, (b1, b1_at), (c1, c1_at), b2, c2 = blocks
    rows, wide = own.shape
    length, width = opened.shape
    half = wide // 2
    last, whole = q is not None, not products
    kept = [g for g, _ in products if g is not None]
    flat_ws = [x for w in ws for x in w] if products else []
    arrays = [own, a, b1, c1, b2, *c2, opened, *kept, *flat_ws]
    arrays += ([] if acc is None else [acc]) + ([q] if last else [])
    outs = [((half, width), F32)] + [((half // sends, width), BF16)] * sends
    if whole:
        outs.append(((length, wide), BF16))
    else:
        outs.append(((length, width), BF16 if last else F32))
    if last:
        outs.append(((width // HEAD, HEAD, HEAD), BF16))

    def kernel(*refs):
        refs = list(refs)
        own_ref, a_ref, b1_ref, c1_ref, b2_ref = [refs.pop(0) for _ in range(5)]
        c2_refs = [refs.pop(0) for _ in c2]
        opened_ref = refs.pop(0)
        kept_refs = [refs.pop(0) for _ in kept]
        w_refs = [[refs.pop(0) for _ in w] for w in ws] if products else []
        acc_ref = None if acc is None else refs.pop(0)
        q_ref = refs.pop(0) if last else None
        del refs[:len(after)]
        keep_ref = refs.pop(0)
        send_refs = [refs.pop(0) for _ in range(sends)]
        third_ref = refs.pop(0)
        qg_ref = refs.pop(0) if last else None
        grad = third_ref if whole else refs.pop(0)
        here = lax.axis_index("tsp")

        def place(ref, at, under=0, column=0):
            count = ref.shape[0]
            grad[pl.ds(pl.multiple_of(at * rows + under, count), count), :] = ref[:, column:column + wide]

        at_end = (here == 0) | (here == 3)
        near, far = jnp.where(here < 2, 2, 1), jnp.where(here < 2, 3, 0)
        place(own_ref, here)
        place(a_ref, here ^ 1)

        @pl.when(at_end)
        def _():
            place(c1_ref, near, 0, c1_at)
            for i, ref in enumerate(c2_refs):
                place(ref, far, i * ref.shape[0])

        @pl.when(jnp.logical_not(at_end))
        def _():
            place(b1_ref, near, 0, b1_at)
            place(b2_ref, far)

        sent = (mm(grad[:, half:], opened_ref[...], TN) * norm).astype(BF16)
        for i, ref in enumerate(send_refs):
            ref[...] = sent[i * ref.shape[0]:(i + 1) * ref.shape[0], :]
        keep_ref[...] = mm(grad[:, :half], opened_ref[...], TN) * norm
        if whole:
            return
        total = None if acc is None else acc_ref[...]
        for g, start in products:
            source = grad if g is None else kept_refs.pop(0)
            piece = source.shape[1] // len(ws)
            rows_of_w = jnp.concatenate([rows_of(refs_here, start, piece) for refs_here in w_refs], axis=0)
            term = mm(source[...], rows_of_w, NN)
            total = term if total is None else total + term
        third_ref[...] = total.astype(third_ref.dtype)
        if last:
            for h, at in enumerate(heads_of(third_ref)):
                qg_ref[h] = mm(q_ref[:, at], third_ref[:, at], TN).astype(BF16)

    return pl.pallas_call(
        kernel,
        in_specs=[VMEM] * len(arrays) + [ANY] * len(after),
        out_specs=[VMEM] * len(outs),
        out_shape=[pltpu.VMEM(shape, kind) for shape, kind in outs],
        scratch_shapes=[] if whole else [pltpu.VMEM((length, wide), BF16)],
        compiler_params=params(),
        name="fold",
    )(*in_vmem(*arrays), *after)


def scatter_step(keep, sends, bit, parts=1):
    came = [swap(x, "ctx", bit) for x in sends]
    half, width = keep.shape[0] // 2, keep.shape[1]

    def body(keep_ref, *refs):
        came_refs, first_ref, second_refs = refs[:len(came)], refs[len(came)], refs[len(came) + 1:]
        first_ref[...] = keep_ref[:half, :] + rows_of(came_refs, 0, half).astype(F32)
        rows = half // parts
        for i, ref in enumerate(second_refs):
            at = half + i * rows
            ref[...] = (keep_ref[at:at + rows, :] + rows_of(came_refs, at, rows).astype(F32)).astype(BF16)

    got = on_vmem(
        body, [((half, width), F32)] + [((half // parts, width), BF16)] * parts, [keep, *came], name="split")
    return got[0], got[1:]


def finish(mine, came, offset, length, target):
    rows, width = sum(x.shape[0] for x in mine), mine[0].shape[1]
    arrays = [*mine, *came]

    def kernel(*refs):
        out_ref, total, sem = refs[-3:]
        ours = rows_of(refs[:len(mine)], 0, rows).astype(F32)
        total[...] = ours + rows_of(refs[len(mine):len(arrays)], 0, rows).astype(F32)
        copy = pltpu.make_async_copy(total, out_ref.at[pl.ds(offset, rows)], sem)
        copy.start()
        copy.wait()

    extra = [] if target is None else [target]
    return pl.pallas_call(
        kernel,
        in_specs=[VMEM] * len(arrays) + [HBM] * len(extra),
        out_specs=HBM,
        out_shape=pltpu.HBM((length, width), F32),
        input_output_aliases={} if target is None else {len(arrays): 0},
        scratch_shapes=[pltpu.VMEM((rows, width), F32), pltpu.SemaphoreType.DMA],
        compiler_params=params(),
        name="finish",
    )(*in_vmem(*arrays), *extra)


def shards(queries, keys, values, attn_out, out_grad, out_weight, block_mask):
    ctx = lax.axis_size("ctx")
    assert lax.axis_size("tsp") == 4 and lax.axis_size("dp") == 2
    _, group_len, width = queries.shape
    seq_len = group_len * ctx
    sc = 1.0 / math.sqrt(HEAD * seq_len)
    norm = 1.0 / math.sqrt(seq_len * lax.axis_size("dp"))
    grad = out_grad[0]
    order = reversed_order(ctx)
    block = grad.shape[1] // ctx
    count = len(EIGHTHS)
    pieces = [block * e // 8 for e in EIGHTHS]
    offsets = [sum(pieces[:i]) for i in range(count)]
    bits = bits_of(ctx)
    top = bits[-1]

    def outer(x):
        return lax.ppermute(x, "tsp", [(0, 1), (1, 0), (2, 3), (3, 2)])

    def inner(x):
        return lax.ppermute(x, "tsp", [(1, 2), (2, 1)])

    def to_ends(x):
        return lax.ppermute(x, "tsp", [(1, 0), (2, 3)])

    def other(x):
        return lax.ppermute(x, "dp", [(0, 1), (1, 0)])

    a_all, b_all = outer(grad), inner(grad)
    parts = list(zip(offsets, pieces))
    single = [[part] for part in parts]
    aligned = all(piece % 128 == 0 for piece in pieces)
    q, k, v, opened, w_here, w_low, w_high, *own = load(
        [(x[0], 0, group_len) for x in (queries, keys, values, attn_out)]
        + [(out_weight, 0, block), (out_weight, 0, block // 2), (out_weight, block // 2, block // 2)],
        [(grad, columns_of(group, order, block)) for group in single] if aligned else [])
    if not aligned:
        own = cut(grad, order, single)

    held = {0: [w_here]}
    for bit in reversed(bits[1:]):
        for j in list(held):
            held[j | bit] = [swap(held[j][0] if j else out_weight, "ctx", bit)]
    for j in list(held):
        rows_here = in_rows(held[j][0], 4) if j else (w_low, w_high)
        held[j | bits[0]] = [swap(x, "ctx", bits[0]) for x in rows_here]
    ws = [held[j] for j in order]

    made, final_form = {"wcore": held[bits[0]]}, {}

    def get(name):
        if name not in made:
            kind, _, number = name.partition("_")
            made[name] = builders[kind](*([int(number)] if number else []))
        return made[name]

    def after(name):
        found = []
        for other_name in AFTER.get(name, ()):
            got = get(other_name)
            found += [got] if isinstance(got, jax.Array) else list(got)
        return found

    def tied(name, array):
        waits = after(name)
        final_form[name] = tie(array, *waits) if waits else array
        return final_form[name]

    def build_cut():
        waits = after("cut")
        return cut(b_all, order, [[parts[i] for i in group] for group in GROUPS], waits), cut(
            a_all, order, single, waits)

    def group_of(i):
        return next(g for g, group in enumerate(GROUPS) if i in group)

    def build_c1(g):
        return to_ends(tied(f"c1_{g}", get("cut")[0][g]))

    def build_b2(i):
        return inner(tied(f"b2_{i}", get("cut")[1][i]))

    def build_c2(i):
        return to_ends(tied(f"c2_{i}", get(f"b2_{i}")))

    def build_early():
        return early(q, k, v, block_mask[0, 0], sc)

    def build_prev():
        return scan_states(get("early")[2], sc, False)[0]

    def build_fold(i):
        last = i == count - 1
        g = group_of(i)
        c2 = get(f"c2_{i}")
        c1 = get(f"c1_{g}")
        at = (offsets[i] - offsets[GROUPS[g][0]]) * ctx
        blocks = (
            own[i], final_form[f"b2_{i}"], (final_form[f"c1_{g}"], at), (c1, at), final_form[f"c2_{i}"], [c2])
        products = [] if i == 0 else [(None, offsets[i])]
        if i == 1:
            products.insert(0, (get("fold_0")[-1], offsets[0]))
        acc = get(f"fold_{i - 1}")[CORE_SENDS[i - 1] + 1] if i > 1 else None
        return fold(
            blocks, opened, norm, ws, products, acc, q if last else None, CORE_SENDS[i], after(f"fold_{i}"))

    def build_send(i):
        got = get(f"fold_{i}")
        keep, sends = got[0], got[1:1 + CORE_SENDS[i]]
        for bit in bits[:-1]:
            keep, sends = scatter_step(keep, sends, bit, TOP_SENDS[i] if bit == bits[-2] else 1)
        keeps[i] = keep
        waits = after(f"send_{i}")
        return [tie(x, *waits) for x in sends] if waits else sends

    def build_mine(i):
        sends = get(f"send_{i}")
        keep, came = keeps[i], [swap(x, "ctx", top) for x in sends]
        rows = keep.shape[0] // LAST_SENDS[i]

        def body(keep_ref, *refs):
            for n, ref in enumerate(refs[len(came):]):
                here = rows_of([keep_ref], n * rows, rows) + rows_of(refs[:len(came)], n * rows, rows).astype(F32)
                ref[...] = here.astype(BF16)

        return on_vmem(
            body, [((rows, width), BF16)] * LAST_SENDS[i], [keep, *came], after=after(f"mine_{i}"), name="mine")

    def build_last(i):
        return [other(x) for x in get(f"mine_{i}")]

    def build_later():
        return scan_states(get(f"fold_{count - 1}")[-1], sc, True)

    def build_late():
        mask, s, _ = get("early")
        og = get(f"fold_{count - 1}")[-2]
        return late(q, k, v, og, s, get("prev"), mask, after("late"))

    def build_final():
        _, dkp, dvp = get("late")
        return final(k, v, get("later")[0], dkp, dvp, after("final"))

    keeps = [None] * count
    builders = {
        "cut": build_cut, "c1": build_c1, "b2": build_b2, "c2": build_c2, "early": build_early, "prev": build_prev,
        "fold": build_fold, "send": build_send, "mine": build_mine, "last": build_last, "later": build_later,
        "qg": lambda: get("later")[1], "late": build_late, "final": build_final,
    }
    grown = None
    for i in range(count):
        grown = finish(get(f"mine_{i}"), get(f"last_{i}"), offsets[i], block, grown)
    dq = get("late")[0]
    dk, dv = get("final")
    return dq[None], dk[None], dv[None], grown


def solution(mesh):
    placed = (
        P("dp", "ctx", "tsp"),
        P("dp", "ctx", "tsp"),
        P("dp", "ctx", "tsp"),
        P("dp", "ctx", "tsp"),
        P("dp", ("ctx", "tsp"), None),
        P("ctx", "tsp"),
        P("dp", "ctx", None, None),
    )
    return jax.shard_map(
        shards,
        mesh=mesh,
        in_specs=placed,
        out_specs=(
            P("dp", "ctx", "tsp"),
            P("dp", "ctx", "tsp"),
            P("dp", "ctx", "tsp"),
            P("ctx", "tsp"),
        ),
        check_vma=False,
    )
```

```python
import functools
import math

import jax
import jax.numpy as jnp
from jax import lax
from jax.experimental import pallas as pl
from jax.experimental.pallas import tpu as pltpu
from jax.sharding import PartitionSpec as P

HEAD = 128
BLK = 64
EIGHTHS = (3, 2, 2, 1)
GROUPS = ((0,), (1, 2, 3))
TOP_SENDS = (2, 1, 1, 1)
LAST_SENDS = (1, 1, 1, 1)
OG_SENDS = 4
AFTER = {
    "cut": ("opened",),
    "c1_1": ("b2_1", "c1_0"),
    "late": ("qg",),
    "mine_2": ("late", "last_1"),
    "fold_1": ("prev",),
    "fold_2": ("c2_3",),
    "fold_3": ("last_0", "mine_1"),
}
F32 = jnp.float32
BF16 = jnp.bfloat16
NT = (((1,), (1,)), ((), ()))
NN = (((1,), (0,)), ((), ()))
TN = (((0,), (0,)), ((), ()))
ANY = pl.BlockSpec(memory_space=pl.ANY)
SMEM = pl.BlockSpec(memory_space=pltpu.SMEM)
VMEM = pl.BlockSpec(memory_space=pltpu.VMEM)
HBM = pl.BlockSpec(memory_space=pltpu.HBM)


def mm(a, b, dims):
    return lax.dot_general(a, b, dims, preferred_element_type=F32)


def params(mebibytes=16):
    return pltpu.CompilerParams(vmem_limit_bytes=mebibytes * 1024 * 1024)


def bits_of(count):
    return [1 << b for b in range(count.bit_length() - 1)]


def reversed_order(count):
    width = count.bit_length() - 1
    return [int(format(p, "b").zfill(width)[::-1], 2) if width else 0 for p in range(count)]


def swap(array, axis, bit):
    count = lax.axis_size(axis)
    return lax.ppermute(array, axis, [(i, i ^ bit) for i in range(count)])


def in_hbm(*arrays):
    return [pltpu.with_memory_space_constraint(x, pltpu.HBM) for x in arrays]


def in_vmem(*arrays):
    return [pltpu.with_memory_space_constraint(x, pltpu.VMEM) for x in arrays]


def tie(array, *after):
    def kernel(*refs):
        pass

    return pl.pallas_call(
        kernel,
        in_specs=[ANY] * (1 + len(after)),
        out_specs=ANY,
        out_shape=jax.ShapeDtypeStruct(array.shape, array.dtype),
        input_output_aliases={0: 0},
        compiler_params=params(1),
        name="tie",
    )(array, *after)


def on_vmem(body, outs, arrays, after=(), name="on_vmem"):
    def kernel(*refs):
        body(*refs[:len(arrays)], *refs[len(arrays) + len(after):])

    return pl.pallas_call(
        kernel,
        in_specs=[VMEM] * len(arrays) + [ANY] * len(after),
        out_specs=[VMEM] * len(outs),
        out_shape=[pltpu.VMEM(shape, kind) for shape, kind in outs],
        compiler_params=params(),
        name=name,
    )(*in_vmem(*arrays), *after)


def load(pieces, cuts=(), after=()):
    sources = [x for x, _, _ in pieces] + [x for x, _ in cuts]
    shapes = [(rows, x.shape[1]) for x, _, rows in pieces]
    shapes += [(x.shape[0], sum(width for _, width in columns(0))) for x, columns in cuts]
    count = len(sources)

    def kernel(*refs):
        refs, targets, sems = refs[:count], refs[count + len(after):-1], refs[-1]
        for i, (_, first, rows) in enumerate(pieces):
            pltpu.make_async_copy(refs[i].at[pl.ds(first, rows)], targets[i], sems.at[i]).start()
        here = lax.axis_index("ctx")
        for i, (_, columns) in enumerate(cuts, len(pieces)):
            at = 0
            for start, width in columns(here):
                pltpu.make_async_copy(
                    refs[i].at[:, pl.ds(pl.multiple_of(start, 128), width)],
                    targets[i].at[:, pl.ds(at, width)], sems.at[i]
                ).start()
                at += width
        for i, target in enumerate(targets):
            pltpu.make_async_copy(target, target, sems.at[i]).wait()

    return pl.pallas_call(
        kernel,
        in_specs=[HBM] * count + [ANY] * len(after),
        out_specs=[VMEM] * count,
        out_shape=[pltpu.VMEM(shape, x.dtype) for shape, x in zip(shapes, sources)],
        scratch_shapes=[pltpu.SemaphoreType.DMA((count,))],
        compiler_params=params(1),
        name="load",
    )(*in_hbm(*sources), *after)


def rows_of(refs, start, size):
    found, at = [], 0
    for ref in refs:
        low, high = max(start, at), min(start + size, at + ref.shape[0])
        if low < high:
            found.append(ref[low - at:high - at, :])
        at += ref.shape[0]
    return found[0] if len(found) == 1 else jnp.concatenate(found, axis=0)


def halves(whole, order, parts):
    rows, model = whole.shape
    block = model // (2 * len(order))

    def columns(flip):
        return lambda here: [((here ^ flip ^ j) * block + offset, piece) for offset, piece in parts for j in order]

    if all(piece % 128 == 0 for _, piece in parts):
        return load([], [(whole, columns(0)), (whole, columns(1))])
    here = lax.axis_index("ctx")
    return [
        jnp.concatenate([lax.dynamic_slice(whole, (0, at), (rows, piece)) for at, piece in columns(flip)(here)], axis=1)
        for flip in (0, 1)
    ]


def stack(pairs, widths, after=()):
    outs = [((2 * x.shape[0], width), x.dtype) for (x, _), cuts in zip(pairs, widths) for width in cuts]

    def body(*refs):
        targets = list(refs[2 * len(pairs):])
        for i, cuts in enumerate(widths):
            rows, column = refs[2 * i].shape[0], 0
            for width in cuts:
                target = targets.pop(0)
                target[:rows, :] = refs[2 * i][:, column:column + width]
                target[rows:, :] = refs[2 * i + 1][:, column:column + width]
                column += width

    got = list(on_vmem(body, outs, [x for pair in pairs for x in pair], after=after, name="stack"))
    return [[got.pop(0) for _ in cuts] for cuts in widths]


def scan_states(state, sc, later):
    shape = state.shape
    bits = bits_of(lax.axis_size("ctx"))
    total, came = state, []
    for bit in bits:
        if bit != bits[0]:
            total, = on_vmem(add_kernel, [(shape, total.dtype)], [total, came[-1]], name="add")
        came.append(swap(total, "ctx", bit))

    def body(*refs):
        here = lax.axis_index("ctx")
        sums = jnp.zeros(shape, F32)
        for bit, ref in zip(bits, refs):
            high = ((here & bit) != 0).astype(F32)
            sums = sums + ref[...].astype(F32) * ((1.0 - high) if later else high)
        refs[-1][...] = (sums * sc).astype(BF16)

    return on_vmem(body, [(shape, BF16)], came, name="states")[0], total


def add_kernel(a_ref, b_ref, out_ref):
    out_ref[...] = (a_ref[...].astype(F32) + b_ref[...].astype(F32)).astype(out_ref.dtype)


def spread(table, length):
    blocks = table.shape[0]
    row = lax.broadcasted_iota(jnp.int32, (length, blocks), 0) // BLK
    pick = (row == lax.broadcasted_iota(jnp.int32, (length, blocks), 1)).astype(BF16)
    chosen = mm(pick, (table == 1).astype(BF16), NN).astype(BF16)
    return mm(chosen, pick, NT)


def heads_of(ref):
    return [slice(h * HEAD, (h + 1) * HEAD) for h in range(ref.shape[1] // HEAD)]


def early(q, k, v, table, sc):
    length, width = q.shape
    heads = width // HEAD

    def body(table_ref, q_ref, k_ref, v_ref, mask_ref, s_ref, kv_ref):
        wide = spread(table_ref[...], length)
        row = lax.broadcasted_iota(jnp.int32, (length, length), 0)
        col = lax.broadcasted_iota(jnp.int32, (length, length), 1)
        inside = (row // BLK == col // BLK) & (row >= col)
        before = (row // BLK > col // BLK) & (wide > 0.5)
        mask_ref[...] = jnp.where(inside | before, sc, 0.0)
        for h, at in enumerate(heads_of(q_ref)):
            k_here = k_ref[:, at]
            s_ref[h] = (mm(q_ref[:, at], k_here, NT) * mask_ref[...]).astype(BF16)
            kv_ref[h] = mm(k_here, v_ref[:, at], TN).astype(BF16)

    return on_vmem(
        body,
        [((length, length), F32), ((heads, length, length), BF16), ((heads, HEAD, HEAD), BF16)],
        [table, q, k, v],
        name="early",
    )


def late_kernel(q_ref, k_ref, v_ref, g_ref, s_ref, prev_ref, mask_ref, *refs):
    dq_ref, dkp_ref, dvp_ref, dq, sem = refs[-5:]
    half = q_ref.shape[0] // 2
    lo, hi = slice(0, half), slice(half, 2 * half)
    for h, at in enumerate(heads_of(q_ref)):
        q, k, v, g = q_ref[:, at], k_ref[:, at], v_ref[:, at], g_ref[:, at]

        def weights(rows, cols):
            return (mm(g[rows], v[cols], NT) * mask_ref[rows, cols]).astype(BF16)

        m00, m10, m11 = weights(lo, lo), weights(hi, lo), weights(hi, hi)
        from_state = mm(g, prev_ref[h], NT)
        dq[lo, at] = (mm(m00, k[lo], NN) + from_state[lo]).astype(BF16)
        dq[hi, at] = (mm(m10, k[lo], NN) + mm(m11, k[hi], NN) + from_state[hi]).astype(BF16)
        dkp_ref[lo, at] = mm(m00, q[lo], TN) + mm(m10, q[hi], TN)
        dkp_ref[hi, at] = mm(m11, q[hi], TN)
        dvp_ref[lo, at] = mm(s_ref[h, :, lo], g, TN)
        dvp_ref[hi, at] = mm(s_ref[h, hi, hi], g[hi], TN)
    copy = pltpu.make_async_copy(dq, dq_ref, sem)
    copy.start()
    copy.wait()


def late(q, k, v, g, s, prev, mask, after):
    shape = q.shape
    return pl.pallas_call(
        late_kernel,
        in_specs=[VMEM] * 7 + [ANY] * len(after),
        out_specs=[HBM, VMEM, VMEM],
        out_shape=[pltpu.HBM(shape, BF16), pltpu.VMEM(shape, F32), pltpu.VMEM(shape, F32)],
        scratch_shapes=[pltpu.VMEM(shape, BF16), pltpu.SemaphoreType.DMA],
        compiler_params=params(),
        name="late",
    )(*in_vmem(q, k, v, g, s, prev, mask), *after)


def final_kernel(k_ref, v_ref, later_ref, dkp_ref, dvp_ref, *refs):
    dk_ref, dv_ref, dk, dv, sems = refs[-5:]
    for h, at in enumerate(heads_of(k_ref)):
        dk[:, at] = (dkp_ref[:, at] + mm(v_ref[:, at], later_ref[h], NT)).astype(BF16)
    copy_k = pltpu.make_async_copy(dk, dk_ref, sems.at[0])
    copy_k.start()
    for h, at in enumerate(heads_of(k_ref)):
        dv[:, at] = (dvp_ref[:, at] + mm(k_ref[:, at], later_ref[h], NN)).astype(BF16)
    copy_v = pltpu.make_async_copy(dv, dv_ref, sems.at[1])
    copy_v.start()
    copy_k.wait()
    copy_v.wait()


def final(k, v, later, dkp, dvp, after):
    shape = k.shape
    return pl.pallas_call(
        final_kernel,
        in_specs=[VMEM] * 5 + [ANY] * len(after),
        out_specs=[HBM, HBM],
        out_shape=[pltpu.HBM(shape, BF16)] * 2,
        scratch_shapes=[pltpu.VMEM(shape, BF16)] * 2 + [pltpu.SemaphoreType.DMA((2,))],
        compiler_params=params(),
        name="final",
    )(*in_vmem(k, v, later, dkp, dvp), *after)


def fold(blocks, opened, norm, ws, start, acc, sends, og_sends, after=()):
    own, a, (b1, b1_at), (c1, c1_at), b2, c2 = blocks
    rows, wide = own.shape[0] // 2, own.shape[1]
    length, width = opened.shape
    half, group = wide // 2, length // 2
    last = og_sends > 0
    arrays = [own, a, b1, c1, b2, c2, opened, *ws] + ([] if acc is None else [acc])
    outs = [((half, width), F32)] + [((half // sends, width), BF16)] * sends
    if last:
        outs += [((group, width), F32)] + [((group // og_sends, width), BF16)] * og_sends
    else:
        outs.append(((length, width), F32))

    def kernel(*refs):
        refs = list(refs)
        own_ref, a_ref, b1_ref, c1_ref, b2_ref, c2_ref, opened_ref = [refs.pop(0) for _ in range(7)]
        w_refs = [refs.pop(0) for _ in ws]
        acc_ref = None if acc is None else refs.pop(0)
        del refs[:len(after)]
        keep_ref = refs.pop(0)
        send_refs = [refs.pop(0) for _ in range(sends)]
        og_ref, *og_refs, grad = refs
        here = lax.axis_index("tsp")

        def place(ref, at, column=0):
            for core in range(2):
                to = pl.ds(pl.multiple_of(core * group + at * rows, rows), rows)
                grad[to, :] = ref[core * rows:(core + 1) * rows, column:column + wide]

        at_end = (here == 0) | (here == 3)
        near, far = jnp.where(here < 2, 2, 1), jnp.where(here < 2, 3, 0)
        place(own_ref, here)
        place(a_ref, here ^ 1)

        @pl.when(at_end)
        def _():
            place(c1_ref, near, c1_at)
            place(c2_ref, far)

        @pl.when(jnp.logical_not(at_end))
        def _():
            place(b1_ref, near, b1_at)
            place(b2_ref, far)

        sent = (mm(grad[:, half:], opened_ref[...], TN) * norm).astype(BF16)
        for i, ref in enumerate(send_refs):
            ref[...] = sent[i * ref.shape[0]:(i + 1) * ref.shape[0], :]
        keep_ref[...] = mm(grad[:, :half], opened_ref[...], TN) * norm
        piece = wide // len(ws)
        rows_of_w = jnp.concatenate([ref[start:start + piece, :] for ref in w_refs], axis=0)
        total = mm(grad[...], rows_of_w, NN)
        if acc is not None:
            total = total + acc_ref[...]
        if last:
            og_ref[...] = total[:group]
            for i, ref in enumerate(og_refs):
                at = group + i * ref.shape[0]
                ref[...] = total[at:at + ref.shape[0]].astype(BF16)
        else:
            og_ref[...] = total

    return pl.pallas_call(
        kernel,
        in_specs=[VMEM] * len(arrays) + [ANY] * len(after),
        out_specs=[VMEM] * len(outs),
        out_shape=[pltpu.VMEM(shape, kind) for shape, kind in outs],
        scratch_shapes=[pltpu.VMEM((length, wide), BF16)],
        compiler_params=params(),
        name="fold",
    )(*in_vmem(*arrays), *after)


def join(kept, came, q, after):
    length, width = kept.shape

    def body(kept_ref, *refs):
        came_refs, q_ref, og_ref, qg_ref = refs[:len(came)], refs[-3], refs[-2], refs[-1]
        og_ref[...] = (kept_ref[...] + rows_of(came_refs, 0, length).astype(F32)).astype(BF16)
        for h, at in enumerate(heads_of(og_ref)):
            qg_ref[h] = mm(q_ref[:, at], og_ref[:, at], TN).astype(BF16)

    return on_vmem(
        body, [((length, width), BF16), ((width // HEAD, HEAD, HEAD), BF16)], [kept, *came, q], after=after, name="join")


def scatter_step(keep, sends, bit, parts=1):
    came = [swap(x, "ctx", bit) for x in sends]
    half, width = keep.shape[0] // 2, keep.shape[1]

    def body(keep_ref, *refs):
        came_refs, first_ref, second_refs = refs[:len(came)], refs[len(came)], refs[len(came) + 1:]
        first_ref[...] = keep_ref[:half, :] + rows_of(came_refs, 0, half).astype(F32)
        rows = half // parts
        for i, ref in enumerate(second_refs):
            at = half + i * rows
            ref[...] = (keep_ref[at:at + rows, :] + rows_of(came_refs, at, rows).astype(F32)).astype(BF16)

    got = on_vmem(
        body, [((half, width), F32)] + [((half // parts, width), BF16)] * parts, [keep, *came], name="split")
    return got[0], got[1:]


def finish(mine, came, offset, length, target):
    rows, width = sum(x.shape[0] for x in mine), mine[0].shape[1]
    arrays = [*mine, *came]

    def kernel(*refs):
        out_ref, total, sem = refs[-3:]
        ours = rows_of(refs[:len(mine)], 0, rows).astype(F32)
        total[...] = ours + rows_of(refs[len(mine):len(arrays)], 0, rows).astype(F32)
        copy = pltpu.make_async_copy(total, out_ref.at[pl.ds(offset, rows)], sem)
        copy.start()
        copy.wait()

    extra = [] if target is None else [target]
    return pl.pallas_call(
        kernel,
        in_specs=[VMEM] * len(arrays) + [HBM] * len(extra),
        out_specs=HBM,
        out_shape=pltpu.HBM((length, width), F32),
        input_output_aliases={} if target is None else {len(arrays): 0},
        scratch_shapes=[pltpu.VMEM((rows, width), F32), pltpu.SemaphoreType.DMA],
        compiler_params=params(),
        name="finish",
    )(*in_vmem(*arrays), *extra)


def shards(queries, keys, values, attn_out, out_grad, out_weight, block_mask):
    ctx = lax.axis_size("ctx")
    assert lax.axis_size("tsp") == 4 and lax.axis_size("dp") == 2
    _, group_len, width = queries.shape
    seq_len = group_len * ctx
    sc = 1.0 / math.sqrt(HEAD * seq_len)
    norm = 1.0 / math.sqrt(seq_len * lax.axis_size("dp"))
    grad = out_grad[0]
    order = [2 * r for r in reversed_order(ctx // 2)]
    block = grad.shape[1] // ctx
    count = len(EIGHTHS)
    pieces = [block * e // 8 for e in EIGHTHS]
    offsets = [sum(pieces[:i]) for i in range(count)]
    wides = [piece * len(order) for piece in pieces]
    bits = bits_of(ctx)
    core, top = bits[0], bits[-1]

    OUTER, INNER = ((0, 1), (1, 0), (2, 3), (3, 2)), ((1, 2), (2, 1))

    def outer(x):
        return lax.ppermute(x, "tsp", OUTER)

    def inner(x):
        return lax.ppermute(x, "tsp", INNER)

    def to_ends(x):
        return lax.ppermute(x, "tsp", [(1, 0), (2, 3)])

    def to_other_core(x, pairs):
        return lax.ppermute(
            x, ("ctx", "tsp"), [(t * 4 + i, (t ^ core) * 4 + j) for t in range(ctx) for i, j in pairs])

    def other(x):
        return lax.ppermute(x, "dp", [(0, 1), (1, 0)])

    same, cross = halves(grad, order, list(zip(offsets, pieces)))
    a_pair = outer(same), to_other_core(cross, OUTER)
    b_pair = inner(same), to_other_core(cross, INNER)
    own_pair = same, swap(cross, "ctx", core)
    q, k, v, opened_here, w_here = load(
        [(x[0], 0, group_len) for x in (queries, keys, values, attn_out)] + [(out_weight, 0, block)], after=own_pair[1:])
    opened_there = swap(opened_here, "ctx", core)

    held = {0: w_here}
    for bit in reversed(bits[1:]):
        for j in list(held):
            held[j | bit] = swap(held[j] if j else out_weight, "ctx", bit)
    ws = [held[j] for j in order]

    made, final_form = {"opened": opened_there}, {}

    def get(name):
        if name not in made:
            kind, _, number = name.partition("_")
            made[name] = builders[kind](*([int(number)] if number else []))
        return made[name]

    def after(name):
        found = []
        for other_name in AFTER.get(name, ()):
            got = get(other_name)
            found += [got] if isinstance(got, jax.Array) else list(got)
        return found

    def tied(name, array):
        waits = after(name)
        final_form[name] = tie(array, *waits) if waits else array
        return final_form[name]

    def build_cut():
        waits = after("cut")
        (opened,), own = stack([(opened_here, opened_there), own_pair], [[width], wides], waits)
        b1, = stack([b_pair], [[sum(wides[i] for i in group) for group in GROUPS]], waits)
        a, = stack([a_pair], [wides], waits)
        return b1, a, own, opened

    def group_of(i):
        return next(g for g, group in enumerate(GROUPS) if i in group)

    def build_c1(g):
        return to_ends(tied(f"c1_{g}", get("cut")[0][g]))

    def build_b2(i):
        return inner(tied(f"b2_{i}", get("cut")[1][i]))

    def build_c2(i):
        return to_ends(tied(f"c2_{i}", get(f"b2_{i}")))

    def build_early():
        return early(q, k, v, block_mask[0, 0], sc)

    def build_prev():
        return scan_states(get("early")[2], sc, False)[0]

    def build_fold(i):
        g = group_of(i)
        c2, c1 = get(f"c2_{i}"), get(f"c1_{g}")
        at = (offsets[i] - offsets[GROUPS[g][0]]) * len(order)
        _, _, own, opened = get("cut")
        blocks = own[i], final_form[f"b2_{i}"], (final_form[f"c1_{g}"], at), (c1, at), final_form[f"c2_{i}"], c2
        acc = get(f"fold_{i - 1}")[1 + TOP_SENDS[i - 1]] if i else None
        return fold(
            blocks, opened, norm, ws, offsets[i], acc, TOP_SENDS[i], OG_SENDS if i == count - 1 else 0,
            after(f"fold_{i}"))

    def build_join():
        kept, *sends = get(f"fold_{count - 1}")[1 + TOP_SENDS[-1]:]
        return join(kept, [swap(x, "ctx", core) for x in sends], q, after("join"))

    def build_send(i):
        got = get(f"fold_{i}")
        keep, sends = got[0], got[1:1 + TOP_SENDS[i]]
        for bit in bits[1:-1]:
            keep, sends = scatter_step(keep, sends, bit)
        keeps[i] = keep
        waits = after(f"send_{i}")
        return [tie(x, *waits) for x in sends] if waits else sends

    def build_mine(i):
        sends = get(f"send_{i}")
        keep, came = keeps[i], [swap(x, "ctx", top) for x in sends]
        rows = keep.shape[0] // LAST_SENDS[i]

        def body(keep_ref, *refs):
            for n, ref in enumerate(refs[len(came):]):
                here = rows_of([keep_ref], n * rows, rows) + rows_of(refs[:len(came)], n * rows, rows).astype(F32)
                ref[...] = here.astype(BF16)

        return on_vmem(
            body, [((rows, width), BF16)] * LAST_SENDS[i], [keep, *came], after=after(f"mine_{i}"), name="mine")

    def build_last(i):
        return [other(x) for x in get(f"mine_{i}")]

    def build_later():
        return scan_states(get("join")[1], sc, True)

    def build_late():
        mask, s, _ = get("early")
        og = get("join")[0]
        return late(q, k, v, og, s, get("prev"), mask, after("late"))

    def build_final():
        _, dkp, dvp = get("late")
        return final(k, v, get("later")[0], dkp, dvp, after("final"))

    keeps = [None] * count
    builders = {
        "cut": build_cut, "c1": build_c1, "b2": build_b2, "c2": build_c2, "early": build_early, "prev": build_prev,
        "fold": build_fold, "join": build_join, "send": build_send, "mine": build_mine, "last": build_last, "later": build_later,
        "qg": lambda: get("later")[1], "late": build_late, "final": build_final,
    }
    grown = None
    for i in range(count):
        grown = finish(get(f"mine_{i}"), get(f"last_{i}"), offsets[i], block, grown)
    dq = get("late")[0]
    dk, dv = get("final")
    return dq[None], dk[None], dv[None], grown


def solution(mesh):
    placed = (
        P("dp", "ctx", "tsp"),
        P("dp", "ctx", "tsp"),
        P("dp", "ctx", "tsp"),
        P("dp", "ctx", "tsp"),
        P("dp", ("ctx", "tsp"), None),
        P("ctx", "tsp"),
        P("dp", "ctx", None, None),
    )
    return jax.shard_map(
        shards,
        mesh=mesh,
        in_specs=placed,
        out_specs=(
            P("dp", "ctx", "tsp"),
            P("dp", "ctx", "tsp"),
            P("dp", "ctx", "tsp"),
            P("ctx", "tsp"),
        ),
        check_vma=False,
    )
```

```python
import functools
import math

import jax
import jax.numpy as jnp
from jax import lax
from jax.experimental import pallas as pl
from jax.experimental.pallas import tpu as pltpu
from jax.sharding import PartitionSpec as P

HEAD = 128
BLK = 64
EIGHTHS = (3, 2, 2, 1)
GROUPS = ((0,), (1, 2, 3))
TOP_SENDS = (2, 1, 1, 1)
LAST_SENDS = (1, 1, 1, 1)
OG_SENDS = 2
AFTER = {
    "cut": ("opened",),
    "c1_1": ("b2_0", "c1_0"),
    "c2_1": ("b2_0",),
    "late": ("qg",),
    "mine_2": ("late", "last_1"),
    "fold_1": ("prev",),
    "fold_2": ("c2_3",),
    "fold_3": ("last_0", "mine_1"),
}
F32 = jnp.float32
BF16 = jnp.bfloat16
NT = (((1,), (1,)), ((), ()))
NN = (((1,), (0,)), ((), ()))
TN = (((0,), (0,)), ((), ()))
ANY = pl.BlockSpec(memory_space=pl.ANY)
SMEM = pl.BlockSpec(memory_space=pltpu.SMEM)
VMEM = pl.BlockSpec(memory_space=pltpu.VMEM)
HBM = pl.BlockSpec(memory_space=pltpu.HBM)


def mm(a, b, dims):
    return lax.dot_general(a, b, dims, preferred_element_type=F32)


def params(mebibytes=16):
    return pltpu.CompilerParams(vmem_limit_bytes=mebibytes * 1024 * 1024)


def bits_of(count):
    return [1 << b for b in range(count.bit_length() - 1)]


def reversed_order(count):
    width = count.bit_length() - 1
    return [int(format(p, "b").zfill(width)[::-1], 2) if width else 0 for p in range(count)]


def swap(array, axis, bit):
    count = lax.axis_size(axis)
    return lax.ppermute(array, axis, [(i, i ^ bit) for i in range(count)])


def in_hbm(*arrays):
    return [pltpu.with_memory_space_constraint(x, pltpu.HBM) for x in arrays]


def in_vmem(*arrays):
    return [pltpu.with_memory_space_constraint(x, pltpu.VMEM) for x in arrays]


def tie(array, *after):
    def kernel(*refs):
        pass

    return pl.pallas_call(
        kernel,
        in_specs=[ANY] * (1 + len(after)),
        out_specs=ANY,
        out_shape=jax.ShapeDtypeStruct(array.shape, array.dtype),
        input_output_aliases={0: 0},
        compiler_params=params(1),
        name="tie",
    )(array, *after)


def on_vmem(body, outs, arrays, after=(), name="on_vmem"):
    def kernel(*refs):
        body(*refs[:len(arrays)], *refs[len(arrays) + len(after):])

    return pl.pallas_call(
        kernel,
        in_specs=[VMEM] * len(arrays) + [ANY] * len(after),
        out_specs=[VMEM] * len(outs),
        out_shape=[pltpu.VMEM(shape, kind) for shape, kind in outs],
        compiler_params=params(),
        name=name,
    )(*in_vmem(*arrays), *after)


def load(pieces, cuts=(), after=()):
    sources = [x for x, _, _ in pieces] + [x for x, _ in cuts]
    shapes = [(rows, x.shape[1]) for x, _, rows in pieces]
    shapes += [(x.shape[0], sum(width for _, width in columns(0))) for x, columns in cuts]
    count = len(sources)

    def kernel(*refs):
        refs, targets, sems = refs[:count], refs[count + len(after):-1], refs[-1]
        for i, (_, first, rows) in enumerate(pieces):
            pltpu.make_async_copy(refs[i].at[pl.ds(first, rows)], targets[i], sems.at[i]).start()
        here = lax.axis_index("ctx")
        for i, (_, columns) in enumerate(cuts, len(pieces)):
            at = 0
            for start, width in columns(here):
                pltpu.make_async_copy(
                    refs[i].at[:, pl.ds(pl.multiple_of(start, 128), width)],
                    targets[i].at[:, pl.ds(at, width)], sems.at[i]
                ).start()
                at += width
        for i, target in enumerate(targets):
            pltpu.make_async_copy(target, target, sems.at[i]).wait()

    return pl.pallas_call(
        kernel,
        in_specs=[HBM] * count + [ANY] * len(after),
        out_specs=[VMEM] * count,
        out_shape=[pltpu.VMEM(shape, x.dtype) for shape, x in zip(shapes, sources)],
        scratch_shapes=[pltpu.SemaphoreType.DMA((count,))],
        compiler_params=params(1),
        name="load",
    )(*in_hbm(*sources), *after)


def rows_of(refs, start, size):
    found, at = [], 0
    for ref in refs:
        low, high = max(start, at), min(start + size, at + ref.shape[0])
        if low < high:
            found.append(ref[low - at:high - at, :])
        at += ref.shape[0]
    return found[0] if len(found) == 1 else jnp.concatenate(found, axis=0)


def halves(whole, order, parts):
    rows, model = whole.shape
    block = model // (2 * len(order))

    def columns(flip):
        return lambda here: [((here ^ flip ^ j) * block + offset, piece) for offset, piece in parts for j in order]

    if all(piece % 128 == 0 for _, piece in parts):
        return load([], [(whole, columns(0)), (whole, columns(1))])
    here = lax.axis_index("ctx")
    return [
        jnp.concatenate([lax.dynamic_slice(whole, (0, at), (rows, piece)) for at, piece in columns(flip)(here)], axis=1)
        for flip in (0, 1)
    ]


def stack(pairs, widths, after=()):
    outs = [((2 * x.shape[0], width), x.dtype) for (x, _), cuts in zip(pairs, widths) for width in cuts]

    def body(*refs):
        targets = list(refs[2 * len(pairs):])
        for i, cuts in enumerate(widths):
            rows, column = refs[2 * i].shape[0], 0
            for width in cuts:
                target = targets.pop(0)
                target[:rows, :] = refs[2 * i][:, column:column + width]
                target[rows:, :] = refs[2 * i + 1][:, column:column + width]
                column += width

    got = list(on_vmem(body, outs, [x for pair in pairs for x in pair], after=after, name="stack"))
    return [[got.pop(0) for _ in cuts] for cuts in widths]


def scan_states(state, sc, later):
    shape = state.shape
    bits = bits_of(lax.axis_size("ctx"))
    total, came = state, []
    for bit in bits:
        if bit != bits[0]:
            total, = on_vmem(add_kernel, [(shape, total.dtype)], [total, came[-1]], name="add")
        came.append(swap(total, "ctx", bit))

    def body(*refs):
        here = lax.axis_index("ctx")
        sums = jnp.zeros(shape, F32)
        for bit, ref in zip(bits, refs):
            high = ((here & bit) != 0).astype(F32)
            sums = sums + ref[...].astype(F32) * ((1.0 - high) if later else high)
        refs[-1][...] = (sums * sc).astype(BF16)

    return on_vmem(body, [(shape, BF16)], came, name="states")[0], total


def add_kernel(a_ref, b_ref, out_ref):
    out_ref[...] = (a_ref[...].astype(F32) + b_ref[...].astype(F32)).astype(out_ref.dtype)


def spread(table, length):
    blocks = table.shape[0]
    row = lax.broadcasted_iota(jnp.int32, (length, blocks), 0) // BLK
    pick = (row == lax.broadcasted_iota(jnp.int32, (length, blocks), 1)).astype(BF16)
    chosen = mm(pick, (table == 1).astype(BF16), NN).astype(BF16)
    return mm(chosen, pick, NT)


def heads_of(ref):
    return [slice(h * HEAD, (h + 1) * HEAD) for h in range(ref.shape[1] // HEAD)]


def early(q, k, v, table, sc):
    length, width = q.shape
    heads = width // HEAD

    def body(table_ref, q_ref, k_ref, v_ref, mask_ref, s_ref, kv_ref):
        wide = spread(table_ref[...], length)
        row = lax.broadcasted_iota(jnp.int32, (length, length), 0)
        col = lax.broadcasted_iota(jnp.int32, (length, length), 1)
        inside = (row // BLK == col // BLK) & (row >= col)
        before = (row // BLK > col // BLK) & (wide > 0.5)
        mask_ref[...] = jnp.where(inside | before, sc, 0.0)
        for h, at in enumerate(heads_of(q_ref)):
            k_here = k_ref[:, at]
            s_ref[h] = (mm(q_ref[:, at], k_here, NT) * mask_ref[...]).astype(BF16)
            kv_ref[h] = mm(k_here, v_ref[:, at], TN).astype(BF16)

    return on_vmem(
        body,
        [((length, length), F32), ((heads, length, length), BF16), ((heads, HEAD, HEAD), BF16)],
        [table, q, k, v],
        name="early",
    )


def late_kernel(q_ref, k_ref, v_ref, g_ref, s_ref, prev_ref, mask_ref, *refs):
    dq_ref, dkp_ref, dvp_ref, dq, sem = refs[-5:]
    half = q_ref.shape[0] // 2
    lo, hi = slice(0, half), slice(half, 2 * half)
    for h, at in enumerate(heads_of(q_ref)):
        q, k, v, g = q_ref[:, at], k_ref[:, at], v_ref[:, at], g_ref[:, at]

        def weights(rows, cols):
            return (mm(g[rows], v[cols], NT) * mask_ref[rows, cols]).astype(BF16)

        m00, m10, m11 = weights(lo, lo), weights(hi, lo), weights(hi, hi)
        from_state = mm(g, prev_ref[h], NT)
        dq[lo, at] = (mm(m00, k[lo], NN) + from_state[lo]).astype(BF16)
        dq[hi, at] = (mm(m10, k[lo], NN) + mm(m11, k[hi], NN) + from_state[hi]).astype(BF16)
        dkp_ref[lo, at] = mm(m00, q[lo], TN) + mm(m10, q[hi], TN)
        dkp_ref[hi, at] = mm(m11, q[hi], TN)
        dvp_ref[lo, at] = mm(s_ref[h, :, lo], g, TN)
        dvp_ref[hi, at] = mm(s_ref[h, hi, hi], g[hi], TN)
    copy = pltpu.make_async_copy(dq, dq_ref, sem)
    copy.start()
    copy.wait()


def late(q, k, v, g, s, prev, mask, after):
    shape = q.shape
    return pl.pallas_call(
        late_kernel,
        in_specs=[VMEM] * 7 + [ANY] * len(after),
        out_specs=[HBM, VMEM, VMEM],
        out_shape=[pltpu.HBM(shape, BF16), pltpu.VMEM(shape, F32), pltpu.VMEM(shape, F32)],
        scratch_shapes=[pltpu.VMEM(shape, BF16), pltpu.SemaphoreType.DMA],
        compiler_params=params(),
        name="late",
    )(*in_vmem(q, k, v, g, s, prev, mask), *after)


def final_kernel(k_ref, v_ref, later_ref, dkp_ref, dvp_ref, *refs):
    dk_ref, dv_ref, dk, dv, sems = refs[-5:]
    for h, at in enumerate(heads_of(k_ref)):
        dk[:, at] = (dkp_ref[:, at] + mm(v_ref[:, at], later_ref[h], NT)).astype(BF16)
    copy_k = pltpu.make_async_copy(dk, dk_ref, sems.at[0])
    copy_k.start()
    for h, at in enumerate(heads_of(k_ref)):
        dv[:, at] = (dvp_ref[:, at] + mm(k_ref[:, at], later_ref[h], NN)).astype(BF16)
    copy_v = pltpu.make_async_copy(dv, dv_ref, sems.at[1])
    copy_v.start()
    copy_k.wait()
    copy_v.wait()


def final(k, v, later, dkp, dvp, after):
    shape = k.shape
    return pl.pallas_call(
        final_kernel,
        in_specs=[VMEM] * 5 + [ANY] * len(after),
        out_specs=[HBM, HBM],
        out_shape=[pltpu.HBM(shape, BF16)] * 2,
        scratch_shapes=[pltpu.VMEM(shape, BF16)] * 2 + [pltpu.SemaphoreType.DMA((2,))],
        compiler_params=params(),
        name="final",
    )(*in_vmem(k, v, later, dkp, dvp), *after)


def fold(blocks, opened, norm, ws, start, acc, sends, og_sends, after=()):
    own, a, (b1, b1_at), (c1, c1_at), b2, c2 = blocks
    rows, wide = own.shape[0] // 2, own.shape[1]
    length, width = opened.shape
    half, group = wide // 2, length // 2
    last = og_sends > 0
    arrays = [own, a, b1, c1, b2, c2, opened, *ws] + ([] if acc is None else [acc])
    outs = [((half, width), F32)] + [((half // sends, width), BF16)] * sends
    if last:
        outs += [((group, width), F32)] + [((group // og_sends, width), F32)] * og_sends
    else:
        outs.append(((length, width), F32))

    def kernel(*refs):
        refs = list(refs)
        own_ref, a_ref, b1_ref, c1_ref, b2_ref, c2_ref, opened_ref = [refs.pop(0) for _ in range(7)]
        w_refs = [refs.pop(0) for _ in ws]
        acc_ref = None if acc is None else refs.pop(0)
        del refs[:len(after)]
        keep_ref = refs.pop(0)
        send_refs = [refs.pop(0) for _ in range(sends)]
        og_ref, *og_refs, grad = refs
        here = lax.axis_index("tsp")

        def place(ref, at, column=0):
            for core in range(2):
                to = pl.ds(pl.multiple_of(core * group + at * rows, rows), rows)
                grad[to, :] = ref[core * rows:(core + 1) * rows, column:column + wide]

        at_end = (here == 0) | (here == 3)
        near, far = jnp.where(here < 2, 2, 1), jnp.where(here < 2, 3, 0)
        place(own_ref, here)
        place(a_ref, here ^ 1)

        @pl.when(at_end)
        def _():
            place(c1_ref, near, c1_at)
            place(c2_ref, far)

        @pl.when(jnp.logical_not(at_end))
        def _():
            place(b1_ref, near, b1_at)
            place(b2_ref, far)

        sent = (mm(grad[:, half:], opened_ref[...], TN) * norm).astype(BF16)
        for i, ref in enumerate(send_refs):
            ref[...] = sent[i * ref.shape[0]:(i + 1) * ref.shape[0], :]
        keep_ref[...] = mm(grad[:, :half], opened_ref[...], TN) * norm
        piece = wide // len(ws)
        rows_of_w = jnp.concatenate([ref[start:start + piece, :] for ref in w_refs], axis=0)
        total = mm(grad[...], rows_of_w, NN)
        if acc is not None:
            total = total + acc_ref[...]
        if last:
            og_ref[...] = total[:group]
            for i, ref in enumerate(og_refs):
                at = group + i * ref.shape[0]
                ref[...] = total[at:at + ref.shape[0]]
        else:
            og_ref[...] = total

    return pl.pallas_call(
        kernel,
        in_specs=[VMEM] * len(arrays) + [ANY] * len(after),
        out_specs=[VMEM] * len(outs),
        out_shape=[pltpu.VMEM(shape, kind) for shape, kind in outs],
        scratch_shapes=[pltpu.VMEM((length, wide), BF16)],
        compiler_params=params(),
        name="fold",
    )(*in_vmem(*arrays), *after)


def join(kept, came, q, after):
    length, width = kept.shape

    def body(kept_ref, *refs):
        came_refs, q_ref, og_ref, qg_ref = refs[:len(came)], refs[-3], refs[-2], refs[-1]
        og_ref[...] = (kept_ref[...] + rows_of(came_refs, 0, length).astype(F32)).astype(BF16)
        for h, at in enumerate(heads_of(og_ref)):
            qg_ref[h] = mm(q_ref[:, at], og_ref[:, at], TN).astype(BF16)

    return on_vmem(
        body, [((length, width), BF16), ((width // HEAD, HEAD, HEAD), BF16)], [kept, *came, q], after=after, name="join")


def scatter_step(keep, sends, bit, parts=1):
    came = [swap(x, "ctx", bit) for x in sends]
    half, width = keep.shape[0] // 2, keep.shape[1]

    def body(keep_ref, *refs):
        came_refs, first_ref, second_refs = refs[:len(came)], refs[len(came)], refs[len(came) + 1:]
        first_ref[...] = keep_ref[:half, :] + rows_of(came_refs, 0, half).astype(F32)
        rows = half // parts
        for i, ref in enumerate(second_refs):
            at = half + i * rows
            ref[...] = (keep_ref[at:at + rows, :] + rows_of(came_refs, at, rows).astype(F32)).astype(BF16)

    got = on_vmem(
        body, [((half, width), F32)] + [((half // parts, width), BF16)] * parts, [keep, *came], name="split")
    return got[0], got[1:]


def finish(mine, came, offset, length, target):
    rows, width = sum(x.shape[0] for x in mine), mine[0].shape[1]
    arrays = [*mine, *came]

    def kernel(*refs):
        out_ref, total, sem = refs[-3:]
        ours = rows_of(refs[:len(mine)], 0, rows).astype(F32)
        total[...] = ours + rows_of(refs[len(mine):len(arrays)], 0, rows).astype(F32)
        copy = pltpu.make_async_copy(total, out_ref.at[pl.ds(offset, rows)], sem)
        copy.start()
        copy.wait()

    extra = [] if target is None else [target]
    return pl.pallas_call(
        kernel,
        in_specs=[VMEM] * len(arrays) + [HBM] * len(extra),
        out_specs=HBM,
        out_shape=pltpu.HBM((length, width), F32),
        input_output_aliases={} if target is None else {len(arrays): 0},
        scratch_shapes=[pltpu.VMEM((rows, width), F32), pltpu.SemaphoreType.DMA],
        compiler_params=params(),
        name="finish",
    )(*in_vmem(*arrays), *extra)


def shards(queries, keys, values, attn_out, out_grad, out_weight, block_mask):
    ctx = lax.axis_size("ctx")
    assert lax.axis_size("tsp") == 4 and lax.axis_size("dp") == 2
    _, group_len, width = queries.shape
    seq_len = group_len * ctx
    sc = 1.0 / math.sqrt(HEAD * seq_len)
    norm = 1.0 / math.sqrt(seq_len * lax.axis_size("dp"))
    grad = out_grad[0]
    order = [2 * r for r in reversed_order(ctx // 2)]
    block = grad.shape[1] // ctx
    count = len(EIGHTHS)
    pieces = [block * e // 8 for e in EIGHTHS]
    offsets = [sum(pieces[:i]) for i in range(count)]
    wides = [piece * len(order) for piece in pieces]
    bits = bits_of(ctx)
    core, top = bits[0], bits[-1]

    OUTER, INNER = ((0, 1), (1, 0), (2, 3), (3, 2)), ((1, 2), (2, 1))

    def outer(x):
        return lax.ppermute(x, "tsp", OUTER)

    def inner(x):
        return lax.ppermute(x, "tsp", INNER)

    def to_ends(x):
        return lax.ppermute(x, "tsp", [(1, 0), (2, 3)])

    def to_other_core(x, pairs):
        return lax.ppermute(
            x, ("ctx", "tsp"), [(t * 4 + i, (t ^ core) * 4 + j) for t in range(ctx) for i, j in pairs])

    def other(x):
        return lax.ppermute(x, "dp", [(0, 1), (1, 0)])

    same, cross = halves(grad, order, list(zip(offsets, pieces)))
    a_pair = outer(same), to_other_core(cross, OUTER)
    b_pair = inner(same), to_other_core(cross, INNER)
    own_pair = same, swap(cross, "ctx", core)
    q, k, v, opened_here, w_here = load(
        [(x[0], 0, group_len) for x in (queries, keys, values, attn_out)] + [(out_weight, 0, block)], after=own_pair[1:])
    opened_there = swap(opened_here, "ctx", core)

    held = {0: w_here}
    for bit in reversed(bits[1:]):
        for j in list(held):
            held[j | bit] = swap(held[j] if j else out_weight, "ctx", bit)
    ws = [held[j] for j in order]

    made, final_form = {"opened": opened_there}, {}

    def get(name):
        if name not in made:
            kind, _, number = name.partition("_")
            made[name] = builders[kind](*([int(number)] if number else []))
        return made[name]

    def after(name):
        found = []
        for other_name in AFTER.get(name, ()):
            got = get(other_name)
            found += [got] if isinstance(got, jax.Array) else list(got)
        return found

    def tied(name, array):
        waits = after(name)
        final_form[name] = tie(array, *waits) if waits else array
        return final_form[name]

    def build_cut():
        waits = after("cut")
        (opened,), own = stack([(opened_here, opened_there), own_pair], [[width], wides], waits)
        b1, = stack([b_pair], [[sum(wides[i] for i in group) for group in GROUPS]], waits)
        a, = stack([a_pair], [wides], waits)
        return b1, a, own, opened

    def group_of(i):
        return next(g for g, group in enumerate(GROUPS) if i in group)

    def build_c1(g):
        return to_ends(tied(f"c1_{g}", get("cut")[0][g]))

    def build_b2(i):
        return inner(tied(f"b2_{i}", get("cut")[1][i]))

    def build_c2(i):
        return to_ends(tied(f"c2_{i}", get(f"b2_{i}")))

    def build_early():
        return early(q, k, v, block_mask[0, 0], sc)

    def build_prev():
        return scan_states(get("early")[2], sc, False)[0]

    def build_fold(i):
        g = group_of(i)
        c2, c1 = get(f"c2_{i}"), get(f"c1_{g}")
        at = (offsets[i] - offsets[GROUPS[g][0]]) * len(order)
        _, _, own, opened = get("cut")
        blocks = own[i], final_form[f"b2_{i}"], (final_form[f"c1_{g}"], at), (c1, at), final_form[f"c2_{i}"], c2
        acc = get(f"fold_{i - 1}")[1 + TOP_SENDS[i - 1]] if i else None
        return fold(
            blocks, opened, norm, ws, offsets[i], acc, TOP_SENDS[i], OG_SENDS if i == count - 1 else 0,
            after(f"fold_{i}"))

    def build_join():
        kept, *sends = get(f"fold_{count - 1}")[1 + TOP_SENDS[-1]:]
        return join(kept, [swap(x, "ctx", core) for x in sends], q, after("join"))

    def build_send(i):
        got = get(f"fold_{i}")
        keep, sends = got[0], got[1:1 + TOP_SENDS[i]]
        for bit in bits[1:-1]:
            keep, sends = scatter_step(keep, sends, bit)
        keeps[i] = keep
        waits = after(f"send_{i}")
        return [tie(x, *waits) for x in sends] if waits else sends

    def build_mine(i):
        sends = get(f"send_{i}")
        keep, came = keeps[i], [swap(x, "ctx", top) for x in sends]
        rows = keep.shape[0] // LAST_SENDS[i]

        def body(keep_ref, *refs):
            for n, ref in enumerate(refs[len(came):]):
                here = rows_of([keep_ref], n * rows, rows) + rows_of(refs[:len(came)], n * rows, rows).astype(F32)
                ref[...] = here.astype(BF16)

        return on_vmem(
            body, [((rows, width), BF16)] * LAST_SENDS[i], [keep, *came], after=after(f"mine_{i}"), name="mine")

    def build_last(i):
        return [other(x) for x in get(f"mine_{i}")]

    def build_later():
        return scan_states(get("join")[1], sc, True)

    def build_late():
        mask, s, _ = get("early")
        og = get("join")[0]
        return late(q, k, v, og, s, get("prev"), mask, after("late"))

    def build_final():
        _, dkp, dvp = get("late")
        return final(k, v, get("later")[0], dkp, dvp, after("final"))

    keeps = [None] * count
    builders = {
        "cut": build_cut, "c1": build_c1, "b2": build_b2, "c2": build_c2, "early": build_early, "prev": build_prev,
        "fold": build_fold, "join": build_join, "send": build_send, "mine": build_mine, "last": build_last, "later": build_later,
        "qg": lambda: get("later")[1], "late": build_late, "final": build_final,
    }
    grown = None
    for i in range(count):
        grown = finish(get(f"mine_{i}"), get(f"last_{i}"), offsets[i], block, grown)
    dq = get("late")[0]
    dk, dv = get("final")
    return dq[None], dk[None], dv[None], grown


def solution(mesh):
    placed = (
        P("dp", "ctx", "tsp"),
        P("dp", "ctx", "tsp"),
        P("dp", "ctx", "tsp"),
        P("dp", "ctx", "tsp"),
        P("dp", ("ctx", "tsp"), None),
        P("ctx", "tsp"),
        P("dp", "ctx", None, None),
    )
    return jax.shard_map(
        shards,
        mesh=mesh,
        in_specs=placed,
        out_specs=(
            P("dp", "ctx", "tsp"),
            P("dp", "ctx", "tsp"),
            P("dp", "ctx", "tsp"),
            P("ctx", "tsp"),
        ),
        check_vma=False,
    )
```

```python
import functools
import math

import jax
import jax.numpy as jnp
from jax import lax
from jax.experimental import pallas as pl
from jax.experimental.pallas import tpu as pltpu
from jax.sharding import PartitionSpec as P

HEAD = 128
BLK = 64
EIGHTHS = (3, 2, 2, 1)
GROUPS = ((0,), (1, 2, 3))
TOP_SENDS = (2, 1, 1, 1)
LAST_SENDS = (1, 1, 1, 1)
OG_SENDS = 2
AFTER = {
    "cut": ("opened",),
    "c1_1": ("b2_0", "c1_0"),
    "c2_1": ("b2_0",),
    "late": ("qg",),
    "mine_2": ("late", "last_1"),
    "fold_1": ("prev",),
    "fold_2": ("c2_3", "b2_3"),
    "fold_3": ("last_0", "mine_1"),
}
F32 = jnp.float32
BF16 = jnp.bfloat16
NT = (((1,), (1,)), ((), ()))
NN = (((1,), (0,)), ((), ()))
TN = (((0,), (0,)), ((), ()))
ANY = pl.BlockSpec(memory_space=pl.ANY)
SMEM = pl.BlockSpec(memory_space=pltpu.SMEM)
VMEM = pl.BlockSpec(memory_space=pltpu.VMEM)
HBM = pl.BlockSpec(memory_space=pltpu.HBM)


def mm(a, b, dims):
    return lax.dot_general(a, b, dims, preferred_element_type=F32)


def params(mebibytes=16):
    return pltpu.CompilerParams(vmem_limit_bytes=mebibytes * 1024 * 1024)


def bits_of(count):
    return [1 << b for b in range(count.bit_length() - 1)]


def reversed_order(count):
    width = count.bit_length() - 1
    return [int(format(p, "b").zfill(width)[::-1], 2) if width else 0 for p in range(count)]


def swap(array, axis, bit):
    count = lax.axis_size(axis)
    return lax.ppermute(array, axis, [(i, i ^ bit) for i in range(count)])


def in_hbm(*arrays):
    return [pltpu.with_memory_space_constraint(x, pltpu.HBM) for x in arrays]


def in_vmem(*arrays):
    return [pltpu.with_memory_space_constraint(x, pltpu.VMEM) for x in arrays]


def tie(array, *after):
    def kernel(*refs):
        pass

    return pl.pallas_call(
        kernel,
        in_specs=[ANY] * (1 + len(after)),
        out_specs=ANY,
        out_shape=jax.ShapeDtypeStruct(array.shape, array.dtype),
        input_output_aliases={0: 0},
        compiler_params=params(1),
        name="tie",
    )(array, *after)


def on_vmem(body, outs, arrays, after=(), name="on_vmem"):
    def kernel(*refs):
        body(*refs[:len(arrays)], *refs[len(arrays) + len(after):])

    return pl.pallas_call(
        kernel,
        in_specs=[VMEM] * len(arrays) + [ANY] * len(after),
        out_specs=[VMEM] * len(outs),
        out_shape=[pltpu.VMEM(shape, kind) for shape, kind in outs],
        compiler_params=params(),
        name=name,
    )(*in_vmem(*arrays), *after)


def load(pieces, cuts=(), after=()):
    sources = [x for x, _, _ in pieces] + [x for x, _ in cuts]
    shapes = [(rows, x.shape[1]) for x, _, rows in pieces]
    shapes += [(x.shape[0], sum(width for _, width in columns(0))) for x, columns in cuts]
    count = len(sources)

    def kernel(*refs):
        refs, targets, sems = refs[:count], refs[count + len(after):-1], refs[-1]
        for i, (_, first, rows) in enumerate(pieces):
            pltpu.make_async_copy(refs[i].at[pl.ds(first, rows)], targets[i], sems.at[i]).start()
        here = lax.axis_index("ctx")
        for i, (_, columns) in enumerate(cuts, len(pieces)):
            at = 0
            for start, width in columns(here):
                pltpu.make_async_copy(
                    refs[i].at[:, pl.ds(pl.multiple_of(start, 128), width)],
                    targets[i].at[:, pl.ds(at, width)], sems.at[i]
                ).start()
                at += width
        for i, target in enumerate(targets):
            pltpu.make_async_copy(target, target, sems.at[i]).wait()

    return pl.pallas_call(
        kernel,
        in_specs=[HBM] * count + [ANY] * len(after),
        out_specs=[VMEM] * count,
        out_shape=[pltpu.VMEM(shape, x.dtype) for shape, x in zip(shapes, sources)],
        scratch_shapes=[pltpu.SemaphoreType.DMA((count,))],
        compiler_params=params(1),
        name="load",
    )(*in_hbm(*sources), *after)


def rows_of(refs, start, size):
    found, at = [], 0
    for ref in refs:
        low, high = max(start, at), min(start + size, at + ref.shape[0])
        if low < high:
            found.append(ref[low - at:high - at, :])
        at += ref.shape[0]
    return found[0] if len(found) == 1 else jnp.concatenate(found, axis=0)


def halves(whole, order, parts):
    rows, model = whole.shape
    block = model // (2 * len(order))

    def columns(flip):
        return lambda here: [((here ^ flip ^ j) * block + offset, piece) for offset, piece in parts for j in order]

    if all(piece % 128 == 0 for _, piece in parts):
        return load([], [(whole, columns(0)), (whole, columns(1))])
    here = lax.axis_index("ctx")
    return [
        jnp.concatenate([lax.dynamic_slice(whole, (0, at), (rows, piece)) for at, piece in columns(flip)(here)], axis=1)
        for flip in (0, 1)
    ]


def stack(pairs, widths, after=()):
    outs = [((2 * x.shape[0], width), x.dtype) for (x, _), cuts in zip(pairs, widths) for width in cuts]

    def body(*refs):
        targets = list(refs[2 * len(pairs):])
        for i, cuts in enumerate(widths):
            rows, column = refs[2 * i].shape[0], 0
            for width in cuts:
                target = targets.pop(0)
                target[:rows, :] = refs[2 * i][:, column:column + width]
                target[rows:, :] = refs[2 * i + 1][:, column:column + width]
                column += width

    got = list(on_vmem(body, outs, [x for pair in pairs for x in pair], after=after, name="stack"))
    return [[got.pop(0) for _ in cuts] for cuts in widths]


def scan_states(state, sc, later):
    shape = state.shape
    bits = bits_of(lax.axis_size("ctx"))
    total, came = state, []
    for bit in bits:
        if bit != bits[0]:
            total, = on_vmem(add_kernel, [(shape, total.dtype)], [total, came[-1]], name="add")
        came.append(swap(total, "ctx", bit))

    def body(*refs):
        here = lax.axis_index("ctx")
        sums = jnp.zeros(shape, F32)
        for bit, ref in zip(bits, refs):
            high = ((here & bit) != 0).astype(F32)
            sums = sums + ref[...].astype(F32) * ((1.0 - high) if later else high)
        refs[-1][...] = (sums * sc).astype(BF16)

    return on_vmem(body, [(shape, BF16)], came, name="states")[0], total


def add_kernel(a_ref, b_ref, out_ref):
    out_ref[...] = (a_ref[...].astype(F32) + b_ref[...].astype(F32)).astype(out_ref.dtype)


def spread(table, length):
    blocks = table.shape[0]
    row = lax.broadcasted_iota(jnp.int32, (length, blocks), 0) // BLK
    pick = (row == lax.broadcasted_iota(jnp.int32, (length, blocks), 1)).astype(BF16)
    chosen = mm(pick, (table == 1).astype(BF16), NN).astype(BF16)
    return mm(chosen, pick, NT)


def heads_of(ref):
    return [slice(h * HEAD, (h + 1) * HEAD) for h in range(ref.shape[1] // HEAD)]


def early(q, k, v, table, sc):
    length, width = q.shape
    heads = width // HEAD

    def body(table_ref, q_ref, k_ref, v_ref, mask_ref, s_ref, kv_ref):
        wide = spread(table_ref[...], length)
        row = lax.broadcasted_iota(jnp.int32, (length, length), 0)
        col = lax.broadcasted_iota(jnp.int32, (length, length), 1)
        inside = (row // BLK == col // BLK) & (row >= col)
        before = (row // BLK > col // BLK) & (wide > 0.5)
        mask_ref[...] = jnp.where(inside | before, sc, 0.0)
        for h, at in enumerate(heads_of(q_ref)):
            k_here = k_ref[:, at]
            s_ref[h] = (mm(q_ref[:, at], k_here, NT) * mask_ref[...]).astype(BF16)
            kv_ref[h] = mm(k_here, v_ref[:, at], TN).astype(BF16)

    return on_vmem(
        body,
        [((length, length), F32), ((heads, length, length), BF16), ((heads, HEAD, HEAD), BF16)],
        [table, q, k, v],
        name="early",
    )


def late_kernel(q_ref, k_ref, v_ref, g_ref, s_ref, prev_ref, mask_ref, *refs):
    dq_ref, dkp_ref, dvp_ref, dq, sem = refs[-5:]
    half = q_ref.shape[0] // 2
    lo, hi = slice(0, half), slice(half, 2 * half)
    for h, at in enumerate(heads_of(q_ref)):
        q, k, v, g = q_ref[:, at], k_ref[:, at], v_ref[:, at], g_ref[:, at]

        def weights(rows, cols):
            return (mm(g[rows], v[cols], NT) * mask_ref[rows, cols]).astype(BF16)

        m00, m10, m11 = weights(lo, lo), weights(hi, lo), weights(hi, hi)
        from_state = mm(g, prev_ref[h], NT)
        dq[lo, at] = (mm(m00, k[lo], NN) + from_state[lo]).astype(BF16)
        dq[hi, at] = (mm(m10, k[lo], NN) + mm(m11, k[hi], NN) + from_state[hi]).astype(BF16)
        dkp_ref[lo, at] = mm(m00, q[lo], TN) + mm(m10, q[hi], TN)
        dkp_ref[hi, at] = mm(m11, q[hi], TN)
        dvp_ref[lo, at] = mm(s_ref[h, :, lo], g, TN)
        dvp_ref[hi, at] = mm(s_ref[h, hi, hi], g[hi], TN)
    copy = pltpu.make_async_copy(dq, dq_ref, sem)
    copy.start()
    copy.wait()


def late(q, k, v, g, s, prev, mask, after):
    shape = q.shape
    return pl.pallas_call(
        late_kernel,
        in_specs=[VMEM] * 7 + [ANY] * len(after),
        out_specs=[HBM, VMEM, VMEM],
        out_shape=[pltpu.HBM(shape, BF16), pltpu.VMEM(shape, F32), pltpu.VMEM(shape, F32)],
        scratch_shapes=[pltpu.VMEM(shape, BF16), pltpu.SemaphoreType.DMA],
        compiler_params=params(),
        name="late",
    )(*in_vmem(q, k, v, g, s, prev, mask), *after)


def final_kernel(k_ref, v_ref, later_ref, dkp_ref, dvp_ref, *refs):
    dk_ref, dv_ref, dk, dv, sems = refs[-5:]
    for h, at in enumerate(heads_of(k_ref)):
        dk[:, at] = (dkp_ref[:, at] + mm(v_ref[:, at], later_ref[h], NT)).astype(BF16)
    copy_k = pltpu.make_async_copy(dk, dk_ref, sems.at[0])
    copy_k.start()
    for h, at in enumerate(heads_of(k_ref)):
        dv[:, at] = (dvp_ref[:, at] + mm(k_ref[:, at], later_ref[h], NN)).astype(BF16)
    copy_v = pltpu.make_async_copy(dv, dv_ref, sems.at[1])
    copy_v.start()
    copy_k.wait()
    copy_v.wait()


def final(k, v, later, dkp, dvp, after):
    shape = k.shape
    return pl.pallas_call(
        final_kernel,
        in_specs=[VMEM] * 5 + [ANY] * len(after),
        out_specs=[HBM, HBM],
        out_shape=[pltpu.HBM(shape, BF16)] * 2,
        scratch_shapes=[pltpu.VMEM(shape, BF16)] * 2 + [pltpu.SemaphoreType.DMA((2,))],
        compiler_params=params(),
        name="final",
    )(*in_vmem(k, v, later, dkp, dvp), *after)


def fold(blocks, opened, norm, ws, start, acc, sends, og_sends, after=()):
    own, a, (b1, b1_at), (c1, c1_at), b2, c2 = blocks
    rows, wide = own.shape[0] // 2, own.shape[1]
    length, width = opened.shape
    half, group = wide // 2, length // 2
    last = og_sends > 0
    arrays = [own, a, b1, c1, b2, c2, opened, *ws] + ([] if acc is None else [acc])
    outs = [((half, width), F32)] + [((half // sends, width), BF16)] * sends
    if last:
        outs += [((group, width), F32)] + [((group // og_sends, width), F32)] * og_sends
    else:
        outs.append(((length, width), F32))

    def kernel(*refs):
        refs = list(refs)
        own_ref, a_ref, b1_ref, c1_ref, b2_ref, c2_ref, opened_ref = [refs.pop(0) for _ in range(7)]
        w_refs = [refs.pop(0) for _ in ws]
        acc_ref = None if acc is None else refs.pop(0)
        del refs[:len(after)]
        keep_ref = refs.pop(0)
        send_refs = [refs.pop(0) for _ in range(sends)]
        og_ref, *og_refs, grad = refs
        here = lax.axis_index("tsp")

        def place(ref, at, column=0):
            for core in range(2):
                to = pl.ds(pl.multiple_of(core * group + at * rows, rows), rows)
                grad[to, :] = ref[core * rows:(core + 1) * rows, column:column + wide]

        at_end = (here == 0) | (here == 3)
        near, far = jnp.where(here < 2, 2, 1), jnp.where(here < 2, 3, 0)
        place(own_ref, here)
        place(a_ref, here ^ 1)

        @pl.when(at_end)
        def _():
            place(c1_ref, near, c1_at)
            place(c2_ref, far)

        @pl.when(jnp.logical_not(at_end))
        def _():
            place(b1_ref, near, b1_at)
            place(b2_ref, far)

        sent = (mm(grad[:, half:], opened_ref[...], TN) * norm).astype(BF16)
        for i, ref in enumerate(send_refs):
            ref[...] = sent[i * ref.shape[0]:(i + 1) * ref.shape[0], :]
        keep_ref[...] = mm(grad[:, :half], opened_ref[...], TN) * norm
        piece = wide // len(ws)
        rows_of_w = jnp.concatenate([ref[start:start + piece, :] for ref in w_refs], axis=0)
        total = mm(grad[...], rows_of_w, NN)
        if acc is not None:
            total = total + acc_ref[...]
        if last:
            og_ref[...] = total[:group]
            for i, ref in enumerate(og_refs):
                at = group + i * ref.shape[0]
                ref[...] = total[at:at + ref.shape[0]]
        else:
            og_ref[...] = total

    return pl.pallas_call(
        kernel,
        in_specs=[VMEM] * len(arrays) + [ANY] * len(after),
        out_specs=[VMEM] * len(outs),
        out_shape=[pltpu.VMEM(shape, kind) for shape, kind in outs],
        scratch_shapes=[pltpu.VMEM((length, wide), BF16)],
        compiler_params=params(),
        name="fold",
    )(*in_vmem(*arrays), *after)


def join(kept, came, q, after):
    length, width = kept.shape

    def body(kept_ref, *refs):
        came_refs, q_ref, og_ref, qg_ref = refs[:len(came)], refs[-3], refs[-2], refs[-1]
        og_ref[...] = (kept_ref[...] + rows_of(came_refs, 0, length).astype(F32)).astype(BF16)
        for h, at in enumerate(heads_of(og_ref)):
            qg_ref[h] = mm(q_ref[:, at], og_ref[:, at], TN).astype(BF16)

    return on_vmem(
        body, [((length, width), BF16), ((width // HEAD, HEAD, HEAD), BF16)], [kept, *came, q], after=after, name="join")


def scatter_step(keep, sends, bit, parts=1):
    came = [swap(x, "ctx", bit) for x in sends]
    half, width = keep.shape[0] // 2, keep.shape[1]

    def body(keep_ref, *refs):
        came_refs, first_ref, second_refs = refs[:len(came)], refs[len(came)], refs[len(came) + 1:]
        first_ref[...] = keep_ref[:half, :] + rows_of(came_refs, 0, half).astype(F32)
        rows = half // parts
        for i, ref in enumerate(second_refs):
            at = half + i * rows
            ref[...] = (keep_ref[at:at + rows, :] + rows_of(came_refs, at, rows).astype(F32)).astype(BF16)

    got = on_vmem(
        body, [((half, width), F32)] + [((half // parts, width), BF16)] * parts, [keep, *came], name="split")
    return got[0], got[1:]


def finish(mine, came, offset, length, target):
    rows, width = sum(x.shape[0] for x in mine), mine[0].shape[1]
    arrays = [*mine, *came]

    def kernel(*refs):
        out_ref, total, sem = refs[-3:]
        ours = rows_of(refs[:len(mine)], 0, rows).astype(F32)
        total[...] = ours + rows_of(refs[len(mine):len(arrays)], 0, rows).astype(F32)
        copy = pltpu.make_async_copy(total, out_ref.at[pl.ds(offset, rows)], sem)
        copy.start()
        copy.wait()

    extra = [] if target is None else [target]
    return pl.pallas_call(
        kernel,
        in_specs=[VMEM] * len(arrays) + [HBM] * len(extra),
        out_specs=HBM,
        out_shape=pltpu.HBM((length, width), F32),
        input_output_aliases={} if target is None else {len(arrays): 0},
        scratch_shapes=[pltpu.VMEM((rows, width), F32), pltpu.SemaphoreType.DMA],
        compiler_params=params(),
        name="finish",
    )(*in_vmem(*arrays), *extra)


def shards(queries, keys, values, attn_out, out_grad, out_weight, block_mask):
    ctx = lax.axis_size("ctx")
    assert lax.axis_size("tsp") == 4 and lax.axis_size("dp") == 2
    _, group_len, width = queries.shape
    seq_len = group_len * ctx
    sc = 1.0 / math.sqrt(HEAD * seq_len)
    norm = 1.0 / math.sqrt(seq_len * lax.axis_size("dp"))
    grad = out_grad[0]
    order = [2 * r for r in reversed_order(ctx // 2)]
    block = grad.shape[1] // ctx
    count = len(EIGHTHS)
    pieces = [block * e // 8 for e in EIGHTHS]
    offsets = [sum(pieces[:i]) for i in range(count)]
    wides = [piece * len(order) for piece in pieces]
    bits = bits_of(ctx)
    core, top = bits[0], bits[-1]

    OUTER, INNER = ((0, 1), (1, 0), (2, 3), (3, 2)), ((1, 2), (2, 1))

    def outer(x):
        return lax.ppermute(x, "tsp", OUTER)

    def inner(x):
        return lax.ppermute(x, "tsp", INNER)

    def to_ends(x):
        return lax.ppermute(x, "tsp", [(1, 0), (2, 3)])

    def to_other_core(x, pairs):
        return lax.ppermute(
            x, ("ctx", "tsp"), [(t * 4 + i, (t ^ core) * 4 + j) for t in range(ctx) for i, j in pairs])

    def other(x):
        return lax.ppermute(x, "dp", [(0, 1), (1, 0)])

    same, cross = halves(grad, order, list(zip(offsets, pieces)))
    a_pair = outer(same), to_other_core(cross, OUTER)
    b_pair = inner(same), to_other_core(cross, INNER)
    own_pair = same, swap(cross, "ctx", core)
    q, k, v, opened_here, w_here = load(
        [(x[0], 0, group_len) for x in (queries, keys, values, attn_out)] + [(out_weight, 0, block)], after=own_pair[1:])
    opened_there = swap(opened_here, "ctx", core)

    held = {0: w_here}
    for bit in reversed(bits[1:]):
        for j in list(held):
            held[j | bit] = swap(held[j] if j else out_weight, "ctx", bit)
    ws = [held[j] for j in order]

    made, final_form = {"opened": opened_there}, {}

    def get(name):
        if name not in made:
            kind, _, number = name.partition("_")
            made[name] = builders[kind](*([int(number)] if number else []))
        return made[name]

    def after(name):
        found = []
        for other_name in AFTER.get(name, ()):
            got = get(other_name)
            found += [got] if isinstance(got, jax.Array) else list(got)
        return found

    def tied(name, array):
        waits = after(name)
        final_form[name] = tie(array, *waits) if waits else array
        return final_form[name]

    def build_cut():
        waits = after("cut")
        (opened,), own = stack([(opened_here, opened_there), own_pair], [[width], wides], waits)
        b1, = stack([b_pair], [[sum(wides[i] for i in group) for group in GROUPS]], waits)
        a, = stack([a_pair], [wides], waits)
        return b1, a, own, opened

    def group_of(i):
        return next(g for g, group in enumerate(GROUPS) if i in group)

    def build_c1(g):
        return to_ends(tied(f"c1_{g}", get("cut")[0][g]))

    def build_b2(i):
        return inner(tied(f"b2_{i}", get("cut")[1][i]))

    def build_c2(i):
        return to_ends(tied(f"c2_{i}", get(f"b2_{i}")))

    def build_early():
        return early(q, k, v, block_mask[0, 0], sc)

    def build_prev():
        return scan_states(get("early")[2], sc, False)[0]

    def build_fold(i):
        g = group_of(i)
        c2, c1 = get(f"c2_{i}"), get(f"c1_{g}")
        at = (offsets[i] - offsets[GROUPS[g][0]]) * len(order)
        _, _, own, opened = get("cut")
        blocks = own[i], final_form[f"b2_{i}"], (final_form[f"c1_{g}"], at), (c1, at), final_form[f"c2_{i}"], c2
        acc = get(f"fold_{i - 1}")[1 + TOP_SENDS[i - 1]] if i else None
        return fold(
            blocks, opened, norm, ws, offsets[i], acc, TOP_SENDS[i], OG_SENDS if i == count - 1 else 0,
            after(f"fold_{i}"))

    def build_join():
        kept, *sends = get(f"fold_{count - 1}")[1 + TOP_SENDS[-1]:]
        return join(kept, [swap(x, "ctx", core) for x in sends], q, after("join"))

    def build_send(i):
        got = get(f"fold_{i}")
        keep, sends = got[0], got[1:1 + TOP_SENDS[i]]
        for bit in bits[1:-1]:
            keep, sends = scatter_step(keep, sends, bit)
        keeps[i] = keep
        waits = after(f"send_{i}")
        return [tie(x, *waits) for x in sends] if waits else sends

    def build_mine(i):
        sends = get(f"send_{i}")
        keep, came = keeps[i], [swap(x, "ctx", top) for x in sends]
        rows = keep.shape[0] // LAST_SENDS[i]

        def body(keep_ref, *refs):
            for n, ref in enumerate(refs[len(came):]):
                here = rows_of([keep_ref], n * rows, rows) + rows_of(refs[:len(came)], n * rows, rows).astype(F32)
                ref[...] = here.astype(BF16)

        return on_vmem(
            body, [((rows, width), BF16)] * LAST_SENDS[i], [keep, *came], after=after(f"mine_{i}"), name="mine")

    def build_last(i):
        return [other(x) for x in get(f"mine_{i}")]

    def build_later():
        return scan_states(get("join")[1], sc, True)

    def build_late():
        mask, s, _ = get("early")
        og = get("join")[0]
        return late(q, k, v, og, s, get("prev"), mask, after("late"))

    def build_final():
        _, dkp, dvp = get("late")
        return final(k, v, get("later")[0], dkp, dvp, after("final"))

    keeps = [None] * count
    builders = {
        "cut": build_cut, "c1": build_c1, "b2": build_b2, "c2": build_c2, "early": build_early, "prev": build_prev,
        "fold": build_fold, "join": build_join, "send": build_send, "mine": build_mine, "last": build_last, "later": build_later,
        "qg": lambda: get("later")[1], "late": build_late, "final": build_final,
    }
    grown = None
    for i in range(count):
        grown = finish(get(f"mine_{i}"), get(f"last_{i}"), offsets[i], block, grown)
    dq = get("late")[0]
    dk, dv = get("final")
    return dq[None], dk[None], dv[None], grown


def solution(mesh):
    placed = (
        P("dp", "ctx", "tsp"),
        P("dp", "ctx", "tsp"),
        P("dp", "ctx", "tsp"),
        P("dp", "ctx", "tsp"),
        P("dp", ("ctx", "tsp"), None),
        P("ctx", "tsp"),
        P("dp", "ctx", None, None),
    )
    return jax.shard_map(
        shards,
        mesh=mesh,
        in_specs=placed,
        out_specs=(
            P("dp", "ctx", "tsp"),
            P("dp", "ctx", "tsp"),
            P("dp", "ctx", "tsp"),
            P("ctx", "tsp"),
        ),
        check_vma=False,
    )
```
